256 devices in a mesh: lon: 32 (over x_lo, z, core), lat: 8 (over x_hi, y).
Axes of the slice: x: 4 (x_hi: 2, x_lo: 2; x = x_hi * 2 + x_lo), y: 4, z: 8, core: 2. Of those that a mesh axis runs over, the one named last changes fastest.
Arguments:
- thermal_field: float32 [16, 512, 4096], P(None, 'lat', 'lon'), may hold values from -6 to 6
- elevation_now: float32 [512, 4096], P('lat', 'lon'), may hold values from -6 to 6
- elevation_prior: float32 [512, 4096], P('lat', 'lon'), may hold values from -6 to 6
- liquid_indicator: int32 [16, 512, 4096], P(None, 'lat', 'lon'), may hold values from 0 to 1, as said below
- seabed_depth: int32 [512, 4096], P('lat', 'lon'), may hold values from 0 to 16
- mixing_coefficients: float32 [16], replicated, may hold values from 0.03 to 0.2
- stencil_filter_matrices: bfloat16 [9, 128, 16], replicated, may hold values from -0.5 to 0.5
- inner_projection_matrix: bfloat16 [512, 128], replicated, may hold values from -0.5 to 0.5
- closing_projection_matrix: bfloat16 [16, 512], replicated, may hold values from -0.25 to 0.25
Outputs:
- corrected: float32 [16, 512, 4096], P(None, 'lat', 'lon')
- eta_out: float32 [512, 4096], P('lat', 'lon')
- eta_mid: float32 [512, 4096], P('lat', 'lon')
The draws below stay inside these ranges and needn't reach their ends.
Inputs may be any that keep to these rules, and one draw needn't show every extreme that they name: `liquid_indicator`: 1 for water, 0 for land; whole continents of land span every level.
All inputs are finite; a program needn't handle non-finite values.
Results may differ from the reference program's by a relative error of at most 0.00033.
Values may be sent and summed in bfloat16 or wider, within the bound.
No kernel may reach another device: no remote copies, remote signals or barrier semaphores. Data moves between devices by JAX's collectives and lax.ppermute only.
A program may use at most 128 MiB of HBM per device.

```python
import math
import jax
import jax.numpy as jnp
from jax import lax

DEPTH_LAYERS = 16
SUB = 8
CH1 = 128
CH2 = 512
PARALLEL_TOTAL = 512
MERIDIAN_TOTAL = 4096


def draw_liquid_indicator(key, part):
    key = jax.random.fold_in(key, 11)
    subkeys = jax.random.split(key, 4)
    row_index = jnp.arange(PARALLEL_TOTAL, dtype=jnp.int32)[None, :, None]
    col_index = jnp.arange(MERIDIAN_TOTAL, dtype=jnp.int32)[None, None, :]
    landed = jnp.zeros((1, PARALLEL_TOTAL, MERIDIAN_TOTAL), jnp.int32)
    spans = (MERIDIAN_TOTAL // 4, MERIDIAN_TOTAL // 6, MERIDIAN_TOTAL // 8)
    for which in range(3):
        anchor = jax.random.randint(subkeys[which], (2,), 0, 1 << 20)
        west_edge = anchor[0] % MERIDIAN_TOTAL
        south_edge = anchor[1] % (PARALLEL_TOTAL // 4 + 1)
        inside_lon = (col_index - west_edge) % MERIDIAN_TOTAL < spans[which]
        inside_lat = (row_index >= south_edge) & (row_index < south_edge + PARALLEL_TOTAL * 5 // 8)
        landed = jnp.maximum(landed, (inside_lon & inside_lat).astype(jnp.int32))
    holes = (jax.random.randint(subkeys[3], (DEPTH_LAYERS, PARALLEL_TOTAL, MERIDIAN_TOTAL), 0, 10) > 0).astype(jnp.int32)
    return (1 - landed) * holes


def plant(values, key, least, top_value):
    dims = values.shape
    index_at = [jax.random.randint(jax.random.fold_in(key, axis), (), 0, dims[axis]) for axis in range(len(dims))]
    values = values.at[tuple(index_at)].set(least)
    longest = dims.index(max(dims))
    index_at[longest] = (index_at[longest] + 1) % dims[longest]
    return values.at[tuple(index_at)].set(top_value)


def block_levels(stream_key, dims, cuts, least, high):
    def one(position, shards_of):
        heights = jax.random.uniform(jax.random.fold_in(jax.random.fold_in(stream_key, 6), position), (shards_of,), jnp.float32, least / len(cuts), high / len(cuts))
        return jnp.repeat(jnp.exp(heights), dims[position] // shards_of).reshape((-1,) + (1,) * (len(dims) - position - 1))

    level = one(*cuts[0])
    for cut in cuts[1:]:
        level = level * one(*cut)
    return level


def bell_draw(own_key, shape, spread, most, shards=(), kind=jnp.bfloat16):
    values = spread * jax.random.normal(own_key, shape, jnp.float32)
    if shards:
        values = values * block_levels(own_key, shape, shards, -0.22, 0.18)
    return jnp.clip(values, -most, most).astype(kind)


def setup_inputs(seed: int = 0) -> dict:
    arg_keys = jax.random.split(jax.random.key(seed), 10)
    return {
        "thermal_field": bell_draw(arg_keys[0], (DEPTH_LAYERS, PARALLEL_TOTAL, MERIDIAN_TOTAL), 1.0, 6.0, ((1, 8), (2, 32)), jnp.float32),
        "elevation_now": bell_draw(arg_keys[1], (PARALLEL_TOTAL, MERIDIAN_TOTAL), 1.0, 6.0, ((0, 8), (1, 32)), jnp.float32),
        "elevation_prior": bell_draw(arg_keys[2], (PARALLEL_TOTAL, MERIDIAN_TOTAL), 1.0, 6.0, ((0, 8), (1, 32)), jnp.float32),
        "liquid_indicator": draw_liquid_indicator(jax.random.fold_in(arg_keys[9], 71), 0),
        "seabed_depth": plant(jax.random.randint(arg_keys[4], (PARALLEL_TOTAL, MERIDIAN_TOTAL), 0, DEPTH_LAYERS + 1), jax.random.fold_in(arg_keys[4], 1), 0, DEPTH_LAYERS).astype(jnp.int32),
        "mixing_coefficients": jnp.clip(jnp.exp(jax.random.uniform(arg_keys[5], (DEPTH_LAYERS,), jnp.float32, math.log(0.03), math.log(0.2))), 0.03, 0.2),
        "stencil_filter_matrices": bell_draw(arg_keys[6], (9, CH1, DEPTH_LAYERS), (9 * DEPTH_LAYERS) ** -0.5, 0.5),
        "inner_projection_matrix": bell_draw(arg_keys[7], (CH2, CH1), CH1 ** -0.5, 0.5),
        "closing_projection_matrix": bell_draw(arg_keys[8], (DEPTH_LAYERS, CH2), CH2 ** -0.5, 0.25),
    }


compass = ((0, 1), (2, 1), (1, 0), (1, 2))


def widen_border(field, width):
    wrapped = jnp.concatenate([field[:, :, -width:], field, field[:, :, :width]], axis=2)
    south_rows = jnp.zeros((field.shape[0], width, wrapped.shape[2]), field.dtype)
    north_rows = jnp.flip(wrapped[:, -width:, :], axis=(1, 2))
    return jnp.concatenate([south_rows, wrapped, north_rows], axis=1)


def scalar_spreading(padded, mixing_coefficients):
    levels = mixing_coefficients.shape[0]
    height = padded.shape[1] - 2
    breadth = padded.shape[2] - 2
    tracer = padded[:levels]
    wetness = padded[levels:]
    centre = tracer[:, 1:-1, 1:-1]
    inflow = jnp.zeros_like(centre)
    for row_shift, col_shift in compass:
        inflow = inflow + wetness[:, row_shift:row_shift + height, col_shift:col_shift + breadth] * (
            tracer[:, row_shift:row_shift + height, col_shift:col_shift + breadth] - centre)
    return centre + mixing_coefficients[:, None, None] * wetness[:, 1:-1, 1:-1] * inflow


def leapfrog(current, earlier, speed, forcing):
    height, breadth = current.shape
    padded_now = jnp.pad(current, 1)
    padded_speed = jnp.pad(speed, 1)
    change = jnp.zeros_like(current)
    for row_shift, col_shift in compass:
        facing = jnp.minimum(speed, padded_speed[row_shift:row_shift + height, col_shift:col_shift + breadth])
        change = change + facing * (padded_now[row_shift:row_shift + height, col_shift:col_shift + breadth] - current)
    active = jnp.where(speed > 0.0, 1.0, 0.0).astype(jnp.float32)
    return active * (2.0 * current - earlier + change + forcing)


def first_layer(window, weights):
    height = window.shape[1] - 2
    breadth = window.shape[2] - 2
    summed = jnp.zeros((weights.shape[1], height, breadth), jnp.float32)
    for kernel_cell in range(9):
        row_shift = kernel_cell // 3
        col_shift = kernel_cell % 3
        summed = summed + jnp.einsum("ok,krx->orx", weights[kernel_cell].astype(jnp.float32),
                                     window[:, row_shift:row_shift + height, col_shift:col_shift + breadth].astype(jnp.float32))
    return jax.nn.gelu(summed, approximate=True).astype(jnp.bfloat16)


def later_layers(hidden, second, third):
    inner = jax.nn.gelu(jnp.einsum("po,orx->prx", second.astype(jnp.float32), hidden.astype(jnp.float32)),
                        approximate=True).astype(jnp.bfloat16)
    return jnp.einsum("kp,prx->krx", third.astype(jnp.float32), inner.astype(jnp.float32)).astype(jnp.bfloat16)


def reference(thermal_field, elevation_now, elevation_prior, liquid_indicator, seabed_depth, mixing_coefficients, stencil_filter_matrices, inner_projection_matrix, closing_projection_matrix):
    levels = mixing_coefficients.shape[0]
    level_index = jnp.arange(levels, dtype=jnp.int32)[:, None, None]
    marine_indicator = liquid_indicator.astype(jnp.float32) * jnp.where(level_index < seabed_depth[None], 1.0, 0.0).astype(jnp.float32)
    warmed_scalar = scalar_spreading(widen_border(jnp.concatenate([thermal_field, marine_indicator], axis=0), 1), mixing_coefficients)
    column = jnp.sum(marine_indicator, axis=0)
    speed = 0.45 * column / levels
    forcing = 0.01 * jnp.sum(marine_indicator * warmed_scalar, axis=0)
    current, earlier = elevation_now, elevation_prior
    for step_index in range(SUB):
        padded = widen_border(jnp.stack([current, earlier, speed, forcing]), 1)
        fresh = leapfrog(padded[0], padded[1], padded[2], padded[3])[1:-1, 1:-1]
        earlier, current = current, fresh
    features = widen_border((marine_indicator * warmed_scalar).astype(jnp.bfloat16), 1)
    band = 16

    def one_band(which):
        window = lax.dynamic_slice_in_dim(features, which * band, band + 2, 1)
        return later_layers(first_layer(window, stencil_filter_matrices), inner_projection_matrix, closing_projection_matrix)

    pieces = lax.map(one_band, jnp.arange(PARALLEL_TOTAL // band, dtype=jnp.int32))
    network = jnp.transpose(pieces, (1, 0, 2, 3)).reshape(levels, PARALLEL_TOTAL, MERIDIAN_TOTAL)
    corrected = warmed_scalar + 0.5 * marine_indicator * network.astype(jnp.float32)
    return corrected, current, earlier
```

```python
import jax
import jax.numpy as jnp
from jax import lax
from jax.experimental import pallas as pl
from jax.experimental.pallas import tpu as pltpu
from jax.sharding import PartitionSpec as P

SUB = 8
F32 = jnp.float32
BF16 = jnp.bfloat16
C0 = 0.7978845608028654
C1 = 0.044715 * C0
VM = pl.BlockSpec(memory_space=pltpu.VMEM)
SM = pl.BlockSpec(memory_space=pltpu.SMEM)
NT = (((1,), (1,)), ((), ()))


def iota(shape, axis):
    return lax.broadcasted_iota(jnp.int32, shape, axis)


def roll(x, shift, axis):
    size = x.shape[axis]
    shift = shift % size
    return x if shift == 0 else pltpu.roll(x, shift, axis)


def lanes_from(x, index):
    return jnp.take_along_axis(x, index, axis=1)


def gelu_twice(x):
    return x + x * jnp.tanh(x * (C0 + C1 * (x * x)))


def call(body, outs, scratch=(), specs=None, flops=0, moved=0, **given):
    return pl.pallas_call(
        body,
        out_shape=outs,
        in_specs=specs,
        out_specs=jax.tree.map(lambda _: VM, outs),
        scratch_shapes=list(scratch),
        compiler_params=pltpu.CompilerParams(vmem_limit_bytes=40 * 1024 * 1024),
        cost_estimate=pl.CostEstimate(flops=flops, bytes_accessed=moved, transcendentals=0),
        **given,
    )


def shape(*dims, dtype=F32):
    return jax.ShapeDtypeStruct(dims, dtype)


def inside(t_ref, l_ref, d_ref, now_ref, prior_ref, mix_ref,
           warm_ref, fk_ref, fc_ref, rt_ref, rf_ref, own_ref, pa_ref, pb_ref):
    lat = lax.axis_index("lat")
    dims = (64, 128)
    lane, row = iota(dims, 1), iota(dims, 0)
    depth = d_ref[...]
    column = jnp.zeros(dims, F32)
    forcing = jnp.zeros(dims, F32)
    rt = jnp.zeros(dims, F32)
    rf = jnp.zeros(dims, F32)

    def around(x):
        east = jnp.where(lane == 127, 0.0, roll(x, 127, 1))
        west = jnp.where(lane == 0, 0.0, roll(x, 1, 1))
        north = jnp.where(row == 63, 0.0, roll(x, 63, 0))
        south = jnp.where(row == 0, 0.0, roll(x, 1, 0))
        return (east + west) + (north + south)

    for k in range(16):
        t = t_ref[k]
        wet = jnp.where(k < depth, l_ref[k].astype(F32), 0.0)
        warm = t + (mix_ref[k] * wet) * (around(wet * t) - t * around(wet))
        feature = wet * warm
        warm_ref[k] = warm
        fk_ref[pl.ds(k, 64, stride=16), :] = feature
        column = column + wet
        forcing = forcing + feature
        rt = jnp.where(lane >> 1 == k, roll(t, 2 * k + 1, 1), rt)
        rt = jnp.where(lane >> 1 == 16 + k, roll(wet, 33 + 2 * k, 1), rt)
        rf = jnp.where(lane >> 3 == k, roll(feature, 8 * k + 4, 1), rf)
    forcing = 0.01 * forcing
    fc_ref[0] = forcing
    fc_ref[1] = column
    rt_ref[...] = rt
    rf_ref[...] = rf

    level = iota((16, 128), 0)

    def edge(r):
        wet = jnp.where(level < d_ref[r : r + 1, :], l_ref[:, r, :].astype(F32), 0.0)
        return t_ref[:, r, :], wet, fk_ref[16 * r : 16 * r + 16, :]

    def payload(r, first):
        t, wet, feature = edge(r)
        own = jnp.concatenate([t, wet], axis=0)
        rows = [x[first : first + 8] for x in (forcing, column, now_ref[...], prior_ref[...], rt)]
        return own, jnp.concatenate([own, feature] + rows, axis=0)

    own_low, low = payload(0, 0)
    own_high, high = payload(63, 56)
    own_ref[...] = jnp.concatenate([own_low, own_high], axis=0)
    even = lat % 2 == 0
    pa_ref[...] = jnp.where(even, high, low)
    pb_ref[...] = jnp.where(even, low, high)

    @pl.when(lat == 7)
    def _():
        small = (8, 128)
        back = 127 - iota(small, 1)
        swap = iota(small, 1) ^ 1
        for i in range(11):
            x = high[8 * i : 8 * i + 8]
            x = lanes_from(x, swap if i == 10 else back)
            if i >= 6:
                x = jnp.concatenate([x[j : j + 1] for j in range(7, -1, -1)], axis=0)
            pb_ref[8 * i : 8 * i + 8, :] = x


def between(pa_ref, pb_ref, own_ref, fk_ref, fc_ref, rt_ref, rf_ref, now_ref, prior_ref, mix_ref,
            e4_ref, fb_ref, dd_ref, rfx_ref, qa_ref, qb_ref):
    lat = lax.axis_index("lat")
    even = lat % 2 == 0
    pa, pb = pa_ref[...], pb_ref[...]
    high = jnp.where(even, pa, pb)
    low = jnp.where(lat == 0, 0.0, jnp.where(even, pb, pa))
    level, lane16 = iota((16, 128), 0), iota((16, 128), 1)
    mix = jnp.zeros((16, 128), F32)
    for k in range(16):
        mix = jnp.where(level == k, mix_ref[k], mix)

    def delta(halo, first):
        t, wet = own_ref[first : first + 16, :], own_ref[first + 16 : first + 32, :]
        return mix * (wet * halo[16:32]) * (halo[0:16] - t)

    d_low, d_high = delta(low, 0), delta(high, 32)
    dd_ref[0:16, :] = d_low
    dd_ref[16:32, :] = d_high
    f_out_low, f_low = low[32:48] - d_low, fk_ref[0:16, :] + d_low
    f_high, f_out_high = fk_ref[1008:1024, :] + d_high, high[32:48] - d_high
    fb_ref[...] = jnp.concatenate([f_out_low, f_low, f_high, f_out_high], axis=0)
    s_low = 0.01 * jnp.sum(d_low, axis=0, keepdims=True)
    s_high = 0.01 * jnp.sum(d_high, axis=0, keepdims=True)

    ext = (80, 128)
    lane, row = iota(ext, 1), iota(ext, 0)

    def extend(i, middle):
        first = 48 + 8 * i
        return jnp.concatenate([low[first : first + 8], middle, high[first : first + 8]], axis=0)

    forcing = extend(0, fc_ref[0])
    forcing = forcing + jnp.where(row == 8, s_low, 0.0) - jnp.where(row == 7, s_low, 0.0)
    forcing = forcing + jnp.where(row == 71, s_high, 0.0) - jnp.where(row == 72, s_high, 0.0)
    fields = [forcing, extend(1, fc_ref[1]), extend(2, now_ref[...]), extend(3, prior_ref[...])]
    mixed = extend(4, rt_ref[...])
    for i, field in enumerate(fields):
        e4_ref[i] = field
        mixed = jnp.where(lane >> 4 == 4 + i, roll(field, 72 + 16 * i, 1), mixed)

    def laid(f):
        x = pltpu.roll(f, 4, 1, stride=8, stride_axis=0)
        return jnp.sum(jnp.where(lane16 >> 3 == level, x, 0.0), axis=0, keepdims=True)

    zero = jnp.zeros((8, 128), F32)
    rf = jnp.concatenate([zero, rf_ref[...], zero], axis=0)
    for at, f in ((7, f_out_low), (8, f_low), (71, f_high), (72, f_out_high)):
        rf = jnp.where(row == at, laid(f), rf)
    rfx_ref[...] = rf

    small = iota((8, 128), 1)

    def columns(side):
        wide = 64 + 16 * ((small - 64) >> 3) + 8 * side + (small & 7)
        index = jnp.where(small < 32, 2 * small + side, jnp.where(small < 64, 0, wide))
        index_f = jnp.where((small >= 32) & (small < 48), 8 * (small - 32) + 3 + side, 0)
        parts = []
        for i in range(10):
            a = lanes_from(mixed[8 * i : 8 * i + 8], index)
            b = lanes_from(rf[8 * i : 8 * i + 8], index_f)
            parts.append(jnp.where((small >= 32) & (small < 48), b, a))
        return jnp.concatenate(parts, axis=0)

    first_core = lax.axis_index("lon") % 2 == 0
    q_east, q_west = columns(0), columns(1)
    qa_ref[...] = jnp.where(first_core, q_east, q_west)
    qb_ref[...] = jnp.where(first_core, q_west, q_east)


def stencil(w1_ref):
    return jnp.concatenate([w1_ref[3 * a + b] for b in range(3) for a in range(3)], axis=1)


def halves(w2_ref, w3_ref):
    return (w2_ref[...].astype(F32) * 0.5).astype(BF16), (w3_ref[...].astype(F32) * 0.5).astype(BF16)


def layers(w1, w2, w3, window):
    h = gelu_twice(jnp.dot(w1, window, preferred_element_type=F32)).astype(BF16)
    total = None
    for m in range(2):
        x = jnp.dot(w2[256 * m : 256 * m + 256], h, preferred_element_type=F32)
        y = gelu_twice(x).astype(BF16)
        part = jnp.dot(w3[:, 256 * m : 256 * m + 256], y, preferred_element_type=F32)
        total = part if total is None else total + part
    return 0.5 * total.astype(BF16).astype(F32)


GROUP = 4


def sweep(w1_ref, w2_ref, w3_ref, g_ref, fw, f0, fe, count, start):
    w1 = stencil(w1_ref)
    w2, w3 = halves(w2_ref, w3_ref)

    def step(g, carry):
        windows = []
        for i in range(GROUP):
            at = pl.multiple_of(16 * start(GROUP * g + i), 16)
            windows.append(jnp.concatenate([f[pl.ds(at, 48), :] for f in (fw, f0, fe)], axis=0))
        net = layers(w1, w2, w3, jnp.concatenate(windows, axis=1))
        for i in range(GROUP):
            at = pl.multiple_of(16 * (GROUP * g + i), 16)
            g_ref[pl.ds(at, 16), :] = net[:, 128 * i : 128 * i + 128]
        return carry

    lax.fori_loop(0, count // GROUP, step, 0)


def put(fw, f0, fe, at, x):
    n = x.shape[0]
    f0[at : at + n, :] = x.astype(BF16)
    fw[at : at + n, :] = roll(x, 1, 1).astype(BF16)
    fe[at : at + n, :] = roll(x, 127, 1).astype(BF16)


def middle_rows(fk_ref, w1_ref, w2_ref, w3_ref, g_ref, fw, f0, fe):
    put(fw, f0, fe, 0, fk_ref[16 * 7 : 16 * 41, :])
    sweep(w1_ref, w2_ref, w3_ref, g_ref, fw, f0, fe, 32, lambda i: i)


def outer_rows(fk_ref, fb_ref, w1_ref, w2_ref, w3_ref, g_ref, fw, f0, fe):
    put(fw, f0, fe, 0, fk_ref[16 * 39 : 16 * 63, :])
    put(fw, f0, fe, 16 * 24, fb_ref[32:64, :])
    put(fw, f0, fe, 16 * 26, fb_ref[0:32, :])
    put(fw, f0, fe, 16 * 28, fk_ref[16 : 16 * 9, :])
    sweep(w1_ref, w2_ref, w3_ref, g_ref, fw, f0, fe, 32, lambda i: i + jnp.where(i >= 24, 2, 0))


def closing(qa_ref, qb_ref, ha_ref, hb_ref, rf_ref, e4_ref, dd_ref, warm_ref, l_ref, d_ref,
            g1_ref, g2_ref, w1_ref, w2_ref, w3_ref, mix_ref, out_ref, eta_ref, mid_ref):
    first_core = lax.axis_index("lon") % 2 == 0
    ext = (80, 128)
    lane, row = iota(ext, 1), iota(ext, 0)
    qa, qb, ha, hb = qa_ref[...], qb_ref[...], ha_ref[...], hb_ref[...]
    q_west, q_east = jnp.where(first_core, qb, qa), jnp.where(first_core, qa, qb)
    h_west, h_east = jnp.where(first_core, hb, ha), jnp.where(first_core, ha, hb)
    mix = jnp.zeros(ext, F32)
    for k in range(16):
        mix = jnp.where(lane == k, mix_ref[k], mix)

    def delta(halo, own):
        return mix * roll(halo * own, 112, 1) * (halo - own)

    d_west, d_east = delta(h_west, q_west), delta(h_east, q_east)

    side = []
    for i in range(4):
        east = roll(h_east, 128 - (64 + 8 * i), 1)
        west = roll(h_west, 56 - 8 * i, 1)
        side.append(jnp.where(lane < 8, east, jnp.where(lane >= 120, west, 0.0)))
    main = [e4_ref[i] for i in range(4)]
    s_west = 0.01 * jnp.sum(d_west, axis=1, keepdims=True)
    s_east = 0.01 * jnp.sum(d_east, axis=1, keepdims=True)
    push = [main[0] + jnp.where(lane == 0, s_west, 0.0) + jnp.where(lane == 127, s_east, 0.0),
            side[0] - jnp.where(lane == 127, s_west, 0.0) - jnp.where(lane == 0, s_east, 0.0)]
    speed = [0.45 * x / 16 for x in (main[1], side[1])]
    current = [main[2], side[2]]
    earlier = [main[3], side[3]]

    def neighbours(pair):
        out = []
        for i in range(2):
            x, other = pair[i], pair[1 - i]
            out.append((roll(jnp.where(lane == 0, other, x), 127, 1),
                        roll(jnp.where(lane == 127, other, x), 1, 1),
                        roll(x, 79, 0), roll(x, 1, 0)))
        return out

    active = [jnp.where(s > 0.0, 1.0, 0.0).astype(F32) for s in speed]
    facing = [[jnp.minimum(s, n) for n in ns] for s, ns in zip(speed, neighbours(speed))]
    for _ in range(SUB):
        fresh = []
        for i, ns in enumerate(neighbours(current)):
            c = current[i]
            change = 2.0 * c - earlier[i] + push[i]
            for f, n in zip(facing[i], ns):
                change = change + f * (n - c)
            fresh.append(active[i] * change)
        current, earlier = fresh, current
    eta_ref[...] = current[0][8:72]
    mid_ref[...] = earlier[0][8:72]

    small = iota((8, 128), 1)
    rf = rf_ref[...]
    index_w = jnp.where(small < 64, 8 * (small & 15) + 3 + (small >> 4), 0)
    index_e = jnp.where(small < 64, 8 * (small & 15) + 1 + (small >> 4), 0)
    f_west = jnp.concatenate([lanes_from(rf[8 * i : 8 * i + 8], index_w) for i in range(10)], axis=0)
    f_east = jnp.concatenate([lanes_from(rf[8 * i : 8 * i + 8], index_e) for i in range(10)], axis=0)
    which = lane >> 4
    f_west = jnp.where(which == 0, roll(h_west, 96, 1) - d_west,
                       f_west + jnp.where(which == 1, roll(d_west, 16, 1), 0.0))
    f_east = jnp.where(which == 3, roll(h_east, 16, 1) - roll(d_east, 48, 1),
                       f_east + jnp.where(which == 2, roll(d_east, 32, 1), 0.0))
    cells = [f_east, roll(f_east, 112, 1), f_west, roll(f_west, 112, 1)]
    w2, w3 = halves(w2_ref, w3_ref)
    blank = jnp.zeros((128, 80), BF16)
    x = jnp.zeros((256, 128), F32)
    for a in range(3):
        window = jnp.concatenate([c[7 + a : 71 + a] for c in cells], axis=0).astype(BF16)
        w = jnp.concatenate([w1_ref[3 * a + b] for b in range(3)] + [blank], axis=1)
        x = x + lax.dot_general(window, w, NT, preferred_element_type=F32)
    h = gelu_twice(x).astype(BF16)
    y = gelu_twice(lax.dot_general(h, w2, NT, preferred_element_type=F32)).astype(BF16)
    w3 = jnp.concatenate([w3, jnp.zeros((112, 512), BF16)], axis=0)
    net = lax.dot_general(y, w3, NT, preferred_element_type=F32)
    net = 0.5 * net.astype(BF16).astype(F32)
    ends = [net[64 * c : 64 * c + 64] for c in range(4)]
    low16 = lane[:64] < 16
    ends[1] = ends[1] + jnp.where(low16, d_east[8:72], 0.0)
    ends[2] = ends[2] + jnp.where(low16, d_west[8:72], 0.0)
    spread = jnp.where(small < 64, small >> 2, 0)
    edges = []
    for i in range(8):
        x = jnp.zeros((8, 128), F32)
        for c in range(4):
            x = jnp.where(small & 3 == c, lanes_from(ends[c][8 * i : 8 * i + 8], spread), x)
        edges.append(x)

    at_edge = (small < 2) | (small >= 126)
    sub = iota((8, 128), 0)
    for i in range(8):
        depth = d_ref[8 * i : 8 * i + 8, :]
        for k in range(16):
            if i == 0:
                g = g2_ref[pl.ds(24 * 16 + k, 8, stride=16), :]
            elif i < 5:
                g = g1_ref[pl.ds((8 * i - 8) * 16 + k, 8, stride=16), :]
            else:
                g = g2_ref[pl.ds((8 * i - 40) * 16 + k, 8, stride=16), :]
            g = jnp.where(at_edge, roll(edges[i], 126 - 4 * k, 1), g)
            wet = jnp.where(k < depth, l_ref[k, 8 * i : 8 * i + 8, :].astype(F32), 0.0)
            y = warm_ref[k, 8 * i : 8 * i + 8, :] + wet * g
            if i == 0:
                y = y + jnp.where(sub == 0, dd_ref[k : k + 1, :], 0.0)
            if i == 7:
                y = y + jnp.where(sub == 7, dd_ref[16 + k : 17 + k, :], 0.0)
            out_ref[k, 8 * i : 8 * i + 8, :] = y


def partners(partner):
    pairs = []
    for lon in range(32):
        for lat in range(8):
            to = partner(lon, lat)
            pairs.append((8 * lon + lat, 8 * (to[0] % 32) + to[1]))
    return pairs


LAT_A = partners(lambda lon, lat: (lon, lat ^ 1))
LAT_B = partners(
    lambda lon, lat: (31 - lon, 7) if lat == 7 else (lon ^ 1, 0) if lat == 0 else (lon, lat + 1 if lat % 2 else lat - 1)
)
LON_A = partners(lambda lon, lat: (lon ^ 1, lat))
LON_B = partners(lambda lon, lat: (lon + 1 if lon % 2 else lon - 1, lat))


def swap(x, pairs):
    return lax.ppermute(x, ("lon", "lat"), pairs)


def on_device(t, now, prior, liquid, depth, mix, w1, w2, w3):
    warm, fk, fc, rt, rf, own, pa, pb = call(
        inside,
        (shape(16, 64, 128), shape(1024, 128), shape(2, 64, 128), shape(64, 128), shape(64, 128),
         shape(64, 128), shape(88, 128), shape(88, 128)),
        specs=[VM] * 5 + [SM], name="inside", flops=10**7, moved=2 * 10**6,
    )(t, liquid, depth, now, prior, mix)
    ra, rb = swap(pa, LAT_A), swap(pb, LAT_B)
    plane = [pltpu.VMEM((36 * 16, 128), BF16)] * 3
    g1 = call(middle_rows, shape(512, 128), scratch=plane, specs=[VM] * 4, name="middle_rows",
              flops=8 * 10**8, moved=10**6)(fk, w1, w2, w3)
    e4, fb, dd, rfx, qa, qb = call(
        between,
        (shape(4, 80, 128), shape(64, 128), shape(32, 128), shape(80, 128), shape(80, 128), shape(80, 128)),
        specs=[VM] * 9 + [SM], name="between", flops=10**7, moved=10**6,
    )(ra, rb, own, fk, fc, rt, rf, now, prior, mix)
    ha, hb = swap(qa, LON_A), swap(qb, LON_B)
    g2 = call(outer_rows, shape(512, 128), scratch=plane, specs=[VM] * 5, name="outer_rows",
              flops=8 * 10**8, moved=10**6)(fk, fb, w1, w2, w3)
    return call(
        closing,
        (shape(16, 64, 128), shape(64, 128), shape(64, 128)),
        specs=[VM] * 15 + [SM], name="closing", flops=10**8, moved=3 * 10**6,
    )(qa, qb, ha, hb, rfx, e4, dd, warm, liquid, depth, g1, g2, w1, w2, w3, mix)


def solution(mesh):
    wide, flat = P(None, "lat", "lon"), P("lat", "lon")
    return jax.shard_map(
        on_device,
        mesh=mesh,
        in_specs=(wide, flat, flat, wide, flat, P(), P(), P(), P()),
        out_specs=(wide, flat, flat),
        check_vma=False,
    )
```

```python
import jax
import jax.numpy as jnp
from jax import lax
from jax.experimental import pallas as pl
from jax.experimental.pallas import tpu as pltpu
from jax.sharding import PartitionSpec as P

SUB = 8
F32 = jnp.float32
BF16 = jnp.bfloat16
C0 = 0.7978845608028654
C1 = 0.044715 * C0
VM = pl.BlockSpec(memory_space=pltpu.VMEM)
HB = pl.BlockSpec(memory_space=pltpu.HBM)
NT = (((1,), (1,)), ((), ()))


def iota(shape, axis):
    return lax.broadcasted_iota(jnp.int32, shape, axis)


def roll(x, shift, axis):
    size = x.shape[axis]
    shift = shift % size
    return x if shift == 0 else pltpu.roll(x, shift, axis)


def lanes_from(x, index):
    return jnp.take_along_axis(x, index, axis=1)


def gelu_twice(x):
    return x + x * jnp.tanh(x * (C0 + C1 * (x * x)))


def call(body, outs, scratch=(), specs=None, out_specs=None, flops=0, moved=0, room=40, **given):
    return pl.pallas_call(
        body,
        out_shape=outs,
        in_specs=specs,
        out_specs=out_specs or jax.tree.map(lambda _: VM, outs),
        scratch_shapes=list(scratch),
        compiler_params=pltpu.CompilerParams(vmem_limit_bytes=room * 1024 * 1024),
        cost_estimate=pl.CostEstimate(flops=flops, bytes_accessed=moved, transcendentals=0),
        **given,
    )


def shape(*dims, dtype=F32):
    return jax.ShapeDtypeStruct(dims, dtype)


def inside(t_hbm, l_hbm, d_hbm, now_hbm, prior_hbm, mix_hbm,
           warm_ref, wet_ref, fk_ref, fc_ref, rt_ref, rf_ref, own_ref, np_ref, mx_ref, pa_ref, pb_ref,
           t_ref, l_ref, d_ref, mix_ref, sems):
    lat = lax.axis_index("lat")
    copies = [pltpu.make_async_copy(d_hbm, d_ref, sems.at[0]), pltpu.make_async_copy(mix_hbm, mix_ref, sems.at[1])]
    for c in range(4):
        part = pl.ds(4 * c, 4)
        copies.append(pltpu.make_async_copy(t_hbm.at[part], t_ref.at[part], sems.at[2 + 2 * c]))
        copies.append(pltpu.make_async_copy(l_hbm.at[part], l_ref.at[part], sems.at[3 + 2 * c]))
    copies.append(pltpu.make_async_copy(now_hbm, np_ref.at[0], sems.at[10]))
    copies.append(pltpu.make_async_copy(prior_hbm, np_ref.at[1], sems.at[11]))
    for copy in copies:
        copy.start()
    copies[0].wait()
    copies[1].wait()
    dims = (64, 128)
    lane, row = iota(dims, 1), iota(dims, 0)
    depth = d_ref[...]
    column = jnp.zeros(dims, F32)
    forcing = jnp.zeros(dims, F32)
    rt = jnp.zeros(dims, F32)
    rf = jnp.zeros(dims, F32)

    def around(x):
        east = jnp.where(lane == 127, 0.0, roll(x, 127, 1))
        west = jnp.where(lane == 0, 0.0, roll(x, 1, 1))
        north = jnp.where(row == 63, 0.0, roll(x, 63, 0))
        south = jnp.where(row == 0, 0.0, roll(x, 1, 0))
        return (east + west) + (north + south)

    for k in range(16):
        if k % 4 == 0:
            copies[2 + k // 2].wait()
            copies[3 + k // 2].wait()
        t = t_ref[k]
        wet = jnp.where(k < depth, l_ref[k].astype(F32), 0.0)
        wet_ref[k] = wet
        warm = t + (mix_ref[k] * wet) * (around(wet * t) - t * around(wet))
        feature = wet * warm
        warm_ref[k] = warm
        fk_ref[pl.ds(k, 64, stride=16), :] = feature
        column = column + wet
        forcing = forcing + feature
        rt = jnp.where(lane >> 1 == k, roll(t, 2 * k + 1, 1), rt)
        rt = jnp.where(lane >> 1 == 16 + k, roll(wet, 33 + 2 * k, 1), rt)
        rf = jnp.where(lane >> 3 == k, roll(feature, 8 * k + 4, 1), rf)
    forcing = 0.01 * forcing
    fc_ref[0] = forcing
    fc_ref[1] = column
    rt_ref[...] = rt
    rf_ref[...] = rf

    copies[10].wait()
    copies[11].wait()
    level, lane16 = iota((24, 128), 0), iota((24, 128), 1)
    mx = jnp.zeros((24, 128), F32)
    for k in range(16):
        mx = jnp.where((level == k) | ((level == 16) & (lane16 == k)), mix_ref[k], mx)
    mx_ref[...] = mx

    def payload(r, first):
        own = jnp.concatenate([t_ref[:, r, :], wet_ref[:, r, :]], axis=0)
        feature = fk_ref[16 * r : 16 * r + 16, :]
        rows = [x[first : first + 8] for x in (forcing, column, np_ref[0], np_ref[1], rt)]
        return own, jnp.concatenate([own, feature] + rows, axis=0)

    own_low, low = payload(0, 0)
    own_high, high = payload(63, 56)
    own_ref[...] = jnp.concatenate([own_low, own_high], axis=0)
    even = lat % 2 == 0
    pa_ref[...] = jnp.where(even, high, low)
    pb_ref[...] = jnp.where(even, low, high)

    @pl.when(lat == 7)
    def _():
        small = (8, 128)
        back = 127 - iota(small, 1)
        swap = iota(small, 1) ^ 1
        for i in range(11):
            x = high[8 * i : 8 * i + 8]
            x = lanes_from(x, swap if i == 10 else back)
            if i >= 6:
                x = jnp.concatenate([x[j : j + 1] for j in range(7, -1, -1)], axis=0)
            pb_ref[8 * i : 8 * i + 8, :] = x


def between(pa_ref, pb_ref, own_ref, fk_ref, fc_ref, rt_ref, rf_ref, np_ref, mx_ref,
            e4_ref, fb_ref, dd_ref, rfx_ref, qa_ref, qb_ref):
    lat = lax.axis_index("lat")
    even = lat % 2 == 0
    pa, pb = pa_ref[...], pb_ref[...]
    high = jnp.where(even, pa, pb)
    low = jnp.where(lat == 0, 0.0, jnp.where(even, pb, pa))
    level, lane16 = iota((16, 128), 0), iota((16, 128), 1)
    mix = mx_ref[0:16, :]

    def delta(halo, first):
        t, wet = own_ref[first : first + 16, :], own_ref[first + 16 : first + 32, :]
        return mix * (wet * halo[16:32]) * (halo[0:16] - t)

    d_low, d_high = delta(low, 0), delta(high, 32)
    dd_ref[0:16, :] = d_low
    dd_ref[16:32, :] = d_high
    f_out_low, f_low = low[32:48] - d_low, fk_ref[0:16, :] + d_low
    f_high, f_out_high = fk_ref[1008:1024, :] + d_high, high[32:48] - d_high
    fb_ref[...] = jnp.concatenate([f_out_low, f_low, f_high, f_out_high], axis=0)
    s_low = 0.01 * jnp.sum(d_low, axis=0, keepdims=True)
    s_high = 0.01 * jnp.sum(d_high, axis=0, keepdims=True)

    ext = (80, 128)
    lane, row = iota(ext, 1), iota(ext, 0)

    def extend(i, middle):
        first = 48 + 8 * i
        return jnp.concatenate([low[first : first + 8], middle, high[first : first + 8]], axis=0)

    forcing = extend(0, fc_ref[0])
    forcing = forcing + jnp.where(row == 8, s_low, 0.0) - jnp.where(row == 7, s_low, 0.0)
    forcing = forcing + jnp.where(row == 71, s_high, 0.0) - jnp.where(row == 72, s_high, 0.0)
    fields = [forcing, extend(1, fc_ref[1]), extend(2, np_ref[0]), extend(3, np_ref[1])]
    mixed = extend(4, rt_ref[...])
    for i, field in enumerate(fields):
        e4_ref[i] = field
        mixed = jnp.where(lane >> 4 == 4 + i, roll(field, 72 + 16 * i, 1), mixed)

    def laid(f):
        x = pltpu.roll(f, 4, 1, stride=8, stride_axis=0)
        return jnp.sum(jnp.where(lane16 >> 3 == level, x, 0.0), axis=0, keepdims=True)

    zero = jnp.zeros((8, 128), F32)
    rf = jnp.concatenate([zero, rf_ref[...], zero], axis=0)
    for at, f in ((7, f_out_low), (8, f_low), (71, f_high), (72, f_out_high)):
        rf = jnp.where(row == at, laid(f), rf)
    rfx_ref[...] = rf

    small = iota((8, 128), 1)

    def columns(side):
        wide = 64 + 16 * ((small - 64) >> 3) + 8 * side + (small & 7)
        index = jnp.where(small < 32, 2 * small + side, jnp.where(small < 64, 0, wide))
        index_f = jnp.where((small >= 32) & (small < 48), 8 * (small - 32) + 3 + side, 0)
        parts = []
        for i in range(10):
            a = lanes_from(mixed[8 * i : 8 * i + 8], index)
            b = lanes_from(rf[8 * i : 8 * i + 8], index_f)
            parts.append(jnp.where((small >= 32) & (small < 48), b, a))
        return jnp.concatenate(parts, axis=0)

    first_core = lax.axis_index("lon") % 2 == 0
    q_east, q_west = columns(0), columns(1)
    qa_ref[...] = jnp.where(first_core, q_east, q_west)
    qb_ref[...] = jnp.where(first_core, q_west, q_east)


def stencil(w1_ref):
    return jnp.concatenate([w1_ref[3 * a + b] for b in range(3) for a in range(3)], axis=1)


def halves(w2_ref, w3_ref):
    return (w2_ref[...].astype(F32) * 0.5).astype(BF16), (w3_ref[...].astype(F32) * 0.5).astype(BF16)


def layers(w1, w2, w3, window):
    h = gelu_twice(jnp.dot(w1, window, preferred_element_type=F32)).astype(BF16)
    y = gelu_twice(jnp.dot(w2, h, preferred_element_type=F32)).astype(BF16)
    net = jnp.dot(w3, y, preferred_element_type=F32)
    return 0.5 * net.astype(BF16).astype(F32)


GROUP = 16


def sweep(w1_ref, w2_ref, w3_ref, g_ref, fw, f0, fe, starts):
    w1 = stencil(w1_ref)
    w2, w3 = halves(w2_ref, w3_ref)
    for g in range(0, len(starts), GROUP):
        windows = [
            jnp.concatenate([f[16 * at : 16 * at + 48, :] for f in (fw, f0, fe)], axis=0)
            for at in starts[g : g + GROUP]
        ]
        net = layers(w1, w2, w3, jnp.concatenate(windows, axis=1))
        for i in range(GROUP):
            g_ref[16 * (g + i) : 16 * (g + i) + 16, :] = net[:, 128 * i : 128 * i + 128]


def put(fw, f0, fe, at, x):
    n = x.shape[0]
    f0[at : at + n, :] = x.astype(BF16)
    fw[at : at + n, :] = roll(x, 1, 1).astype(BF16)
    fe[at : at + n, :] = roll(x, 127, 1).astype(BF16)


def middle_rows(fk_ref, w1_ref, w2_ref, w3_ref, g_ref, fw, f0, fe):
    put(fw, f0, fe, 0, fk_ref[16 * 7 : 16 * 41, :])
    sweep(w1_ref, w2_ref, w3_ref, g_ref, fw, f0, fe, list(range(32)))


def outer_rows(fk_ref, fb_ref, w1_ref, w2_ref, w3_ref, g_ref, fw, f0, fe):
    put(fw, f0, fe, 0, fk_ref[16 * 39 : 16 * 63, :])
    put(fw, f0, fe, 16 * 24, fb_ref[32:64, :])
    put(fw, f0, fe, 16 * 26, fb_ref[0:32, :])
    put(fw, f0, fe, 16 * 28, fk_ref[16 : 16 * 9, :])
    sweep(w1_ref, w2_ref, w3_ref, g_ref, fw, f0, fe, [i + 2 * (i >= 24) for i in range(32)])


def closing(qa_ref, qb_ref, ha_ref, hb_ref, rf_ref, e4_ref, dd_ref, warm_ref, wet_ref,
            g1_ref, g2_ref, w1_ref, w2_ref, w3_ref, mx_ref, out_hbm, eta_ref, mid_ref, out_ref, sems):
    first_core = lax.axis_index("lon") % 2 == 0
    ext = (80, 128)
    lane, row = iota(ext, 1), iota(ext, 0)
    qa, qb, ha, hb = qa_ref[...], qb_ref[...], ha_ref[...], hb_ref[...]
    q_west, q_east = jnp.where(first_core, qb, qa), jnp.where(first_core, qa, qb)
    h_west, h_east = jnp.where(first_core, hb, ha), jnp.where(first_core, ha, hb)
    mix = mx_ref[16:17, :]

    def delta(halo, own):
        return mix * roll(halo * own, 112, 1) * (halo - own)

    d_west, d_east = delta(h_west, q_west), delta(h_east, q_east)

    side = []
    for i in range(4):
        east = roll(h_east, 128 - (64 + 8 * i), 1)
        west = roll(h_west, 56 - 8 * i, 1)
        side.append(jnp.where(lane < 8, east, jnp.where(lane >= 120, west, 0.0)))
    main = [e4_ref[i] for i in range(4)]
    s_west = 0.01 * jnp.sum(d_west, axis=1, keepdims=True)
    s_east = 0.01 * jnp.sum(d_east, axis=1, keepdims=True)
    push = [main[0] + jnp.where(lane == 0, s_west, 0.0) + jnp.where(lane == 127, s_east, 0.0),
            side[0] - jnp.where(lane == 127, s_west, 0.0) - jnp.where(lane == 0, s_east, 0.0)]
    speed = [0.45 * x / 16 for x in (main[1], side[1])]
    current = [main[2], side[2]]
    earlier = [main[3], side[3]]

    def neighbours(pair):
        out = []
        for i in range(2):
            x, other = pair[i], pair[1 - i]
            out.append((roll(jnp.where(lane == 0, other, x), 127, 1),
                        roll(jnp.where(lane == 127, other, x), 1, 1),
                        roll(x, 79, 0), roll(x, 1, 0)))
        return out

    active = [jnp.where(s > 0.0, 1.0, 0.0).astype(F32) for s in speed]
    facing = [[jnp.minimum(s, n) for n in ns] for s, ns in zip(speed, neighbours(speed))]
    for _ in range(SUB):
        fresh = []
        for i, ns in enumerate(neighbours(current)):
            c = current[i]
            change = 2.0 * c - earlier[i] + push[i]
            for f, n in zip(facing[i], ns):
                change = change + f * (n - c)
            fresh.append(active[i] * change)
        current, earlier = fresh, current
    eta_ref[...] = current[0][8:72]
    mid_ref[...] = earlier[0][8:72]

    small = iota((8, 128), 1)
    rf = rf_ref[...]
    index_w = jnp.where(small < 64, 8 * (small & 15) + 3 + (small >> 4), 0)
    index_e = jnp.where(small < 64, 8 * (small & 15) + 1 + (small >> 4), 0)
    f_west = jnp.concatenate([lanes_from(rf[8 * i : 8 * i + 8], index_w) for i in range(10)], axis=0)
    f_east = jnp.concatenate([lanes_from(rf[8 * i : 8 * i + 8], index_e) for i in range(10)], axis=0)
    which = lane >> 4
    f_west = jnp.where(which == 0, roll(h_west, 96, 1) - d_west,
                       f_west + jnp.where(which == 1, roll(d_west, 16, 1), 0.0))
    f_east = jnp.where(which == 3, roll(h_east, 16, 1) - roll(d_east, 48, 1),
                       f_east + jnp.where(which == 2, roll(d_east, 32, 1), 0.0))
    cells = [f_east, roll(f_east, 112, 1), f_west, roll(f_west, 112, 1)]
    w2, w3 = halves(w2_ref, w3_ref)
    blank = jnp.zeros((128, 80), BF16)
    x = jnp.zeros((256, 128), F32)
    for a in range(3):
        window = jnp.concatenate([c[7 + a : 71 + a] for c in cells], axis=0).astype(BF16)
        w = jnp.concatenate([w1_ref[3 * a + b] for b in range(3)] + [blank], axis=1)
        x = x + lax.dot_general(window, w, NT, preferred_element_type=F32)
    h = gelu_twice(x).astype(BF16)
    y = gelu_twice(lax.dot_general(h, w2, NT, preferred_element_type=F32)).astype(BF16)
    w3 = jnp.concatenate([w3, jnp.zeros((112, 512), BF16)], axis=0)
    net = lax.dot_general(y, w3, NT, preferred_element_type=F32)
    net = 0.5 * net.astype(BF16).astype(F32)
    ends = [net[64 * c : 64 * c + 64] for c in range(4)]
    low16 = lane[:64] < 16
    ends[1] = ends[1] + jnp.where(low16, d_east[8:72], 0.0)
    ends[2] = ends[2] + jnp.where(low16, d_west[8:72], 0.0)
    spread = jnp.where(small < 64, small >> 2, 0)
    edges = []
    for i in range(8):
        x = jnp.zeros((8, 128), F32)
        for c in range(4):
            x = jnp.where(small & 3 == c, lanes_from(ends[c][8 * i : 8 * i + 8], spread), x)
        edges.append(x)

    at_edge = (small < 2) | (small >= 126)
    sub = iota((8, 128), 0)
    copies = []
    for k in range(16):
        for i in range(8):
            if i == 0:
                g = g2_ref[pl.ds(24 * 16 + k, 8, stride=16), :]
            elif i < 5:
                g = g1_ref[pl.ds((8 * i - 8) * 16 + k, 8, stride=16), :]
            else:
                g = g2_ref[pl.ds((8 * i - 40) * 16 + k, 8, stride=16), :]
            g = jnp.where(at_edge, roll(edges[i], 126 - 4 * k, 1), g)
            y = warm_ref[k, 8 * i : 8 * i + 8, :] + wet_ref[k, 8 * i : 8 * i + 8, :] * g
            if i == 0:
                y = y + jnp.where(sub == 0, dd_ref[k : k + 1, :], 0.0)
            if i == 7:
                y = y + jnp.where(sub == 7, dd_ref[16 + k : 17 + k, :], 0.0)
            out_ref[k, 8 * i : 8 * i + 8, :] = y
        if k % 4 == 3:
            part = pl.ds(k - 3, 4)
            copies.append(pltpu.make_async_copy(out_ref.at[part], out_hbm.at[part], sems.at[k // 4]))
            copies[-1].start()
    for copy in copies:
        copy.wait()


def partners(partner):
    pairs = []
    for lon in range(32):
        for lat in range(8):
            to = partner(lon, lat)
            pairs.append((8 * lon + lat, 8 * (to[0] % 32) + to[1]))
    return pairs


LAT_A = partners(lambda lon, lat: (lon, lat ^ 1))
LAT_B = partners(
    lambda lon, lat: (31 - lon, 7) if lat == 7 else (lon ^ 1, 0) if lat == 0 else (lon, lat + 1 if lat % 2 else lat - 1)
)
LON_A = partners(lambda lon, lat: (lon ^ 1, lat))
LON_B = partners(lambda lon, lat: (lon + 1 if lon % 2 else lon - 1, lat))


def swap(x, pairs):
    return lax.ppermute(x, ("lon", "lat"), pairs)


def on_device(t, now, prior, liquid, depth, mix, w1, w2, w3):
    cube, flat, tall = (16, 64, 128), (64, 128), (80, 128)
    warm, wet, fk, fc, rt, rf, own, both, mx, pa, pb = call(
        inside,
        (shape(*cube), shape(*cube), shape(1024, 128), shape(2, 64, 128), shape(*flat), shape(*flat),
         shape(*flat), shape(2, 64, 128), shape(24, 128), shape(88, 128), shape(88, 128)),
        scratch=(pltpu.VMEM(cube, F32), pltpu.VMEM(cube, jnp.int32), pltpu.VMEM(flat, jnp.int32),
                 pltpu.SMEM((16,), F32), pltpu.SemaphoreType.DMA((12,))),
        specs=[HB] * 6, name="inside", flops=10**7, moved=2 * 10**6,
    )(*(pltpu.with_memory_space_constraint(x, pltpu.HBM) for x in (t, liquid, depth, now, prior, mix)))
    ra, rb = swap(pa, LAT_A), swap(pb, LAT_B)
    plane = [pltpu.VMEM((36 * 16, 128), BF16)] * 3
    g1 = call(middle_rows, shape(512, 128), scratch=plane, specs=[VM] * 4, name="middle_rows",
              flops=8 * 10**8, moved=10**6)(fk, w1, w2, w3)
    e4, fb, dd, rfx, qa, qb = call(
        between,
        (shape(4, 80, 128), shape(64, 128), shape(32, 128), shape(*tall), shape(*tall), shape(*tall)),
        specs=[VM] * 9, name="between", flops=10**7, moved=10**6,
    )(ra, rb, own, fk, fc, rt, rf, both, mx)
    ha, hb = swap(qa, LON_A), swap(qb, LON_B)
    g2 = call(outer_rows, shape(512, 128), scratch=plane, specs=[VM] * 5, name="outer_rows",
              flops=8 * 10**8, moved=10**6)(fk, fb, w1, w2, w3)
    return call(
        closing,
        (shape(*cube), shape(*flat), shape(*flat)),
        scratch=(pltpu.VMEM(cube, F32), pltpu.SemaphoreType.DMA((4,))),
        specs=[VM] * 15, out_specs=(HB, VM, VM), name="closing", flops=10**8, moved=3 * 10**6,
    )(qa, qb, ha, hb, rfx, e4, dd, warm, wet, g1, g2, w1, w2, w3, mx)


def solution(mesh):
    wide, flat = P(None, "lat", "lon"), P("lat", "lon")
    return jax.shard_map(
        on_device,
        mesh=mesh,
        in_specs=(wide, flat, flat, wide, flat, P(), P(), P(), P()),
        out_specs=(wide, flat, flat),
        check_vma=False,
    )
```

```python
import functools

import jax
import jax.numpy as jnp
from jax import lax
from jax.experimental import pallas as pl
from jax.experimental.pallas import tpu as pltpu
from jax.sharding import PartitionSpec as P

SUB = 8
F32 = jnp.float32
BF16 = jnp.bfloat16
C0 = 0.7978845608028654
C1 = 0.044715 * C0
DRY = 1e30
VM = pl.BlockSpec(memory_space=pltpu.VMEM)
HB = pl.BlockSpec(memory_space=pltpu.HBM)
NT = (((1,), (1,)), ((), ()))


def iota(shape, axis):
    return lax.broadcasted_iota(jnp.int32, shape, axis)


def roll(x, shift, axis):
    size = x.shape[axis]
    shift = shift % size
    return x if shift == 0 else pltpu.roll(x, shift, axis)


def lanes_from(x, index):
    return jnp.take_along_axis(x, index, axis=1)


def gelu_twice(x):
    return x + x * jnp.tanh(x * (C0 + C1 * (x * x)))


def call(body, outs, scratch=(), specs=None, out_specs=None, flops=0, moved=0, room=40, **given):
    return pl.pallas_call(
        body,
        out_shape=outs,
        in_specs=specs,
        out_specs=out_specs or jax.tree.map(lambda _: VM, outs),
        scratch_shapes=list(scratch),
        compiler_params=pltpu.CompilerParams(vmem_limit_bytes=room * 1024 * 1024),
        cost_estimate=pl.CostEstimate(flops=flops, bytes_accessed=moved, transcendentals=0),
        **given,
    )


def shape(*dims, dtype=F32):
    return jax.ShapeDtypeStruct(dims, dtype)


def inside(t_hbm, l_hbm, d_hbm, now_hbm, prior_hbm, mix_hbm,
           t_ref, warm_ref, wet_ref, fk_ref, fc_ref, own_ref, np_ref, mx_ref, pa_ref, pb_ref,
           l_ref, d_ref, mix_ref, q_ref, sems):
    lat = lax.axis_index("lat")
    copies = [pltpu.make_async_copy(d_hbm, d_ref, sems.at[0]), pltpu.make_async_copy(mix_hbm, mix_ref, sems.at[1])]
    for c in range(4):
        part = pl.ds(4 * c, 4)
        copies.append(pltpu.make_async_copy(t_hbm.at[part], t_ref.at[part], sems.at[2 + 2 * c]))
        copies.append(pltpu.make_async_copy(l_hbm.at[part], l_ref.at[part], sems.at[3 + 2 * c]))
    copies.append(pltpu.make_async_copy(now_hbm, np_ref.at[0], sems.at[10]))
    copies.append(pltpu.make_async_copy(prior_hbm, np_ref.at[1], sems.at[11]))
    for copy in copies:
        copy.start()
    dims = (64, 128)
    lane = iota(dims, 1)
    q_ref[:, 0:8, :] = jnp.full((16, 8, 128), DRY, F32)
    q_ref[:, 72:80, :] = jnp.full((16, 8, 128), DRY, F32)
    column = jnp.zeros(dims, F32)
    forcing = jnp.zeros(dims, F32)
    copies[0].wait()
    copies[1].wait()
    depth = d_ref[...]
    for k in range(16):
        if k % 4 == 0:
            copies[2 + k // 2].wait()
            copies[3 + k // 2].wait()
        t = t_ref[k]
        water = (l_ref[k] > 0) & (k < depth)
        q = jnp.where(water, t, DRY)
        q_ref[k, 8:72, :] = q
        wet = jnp.where(water, 1.0, 0.0).astype(F32)
        wet_ref[k] = wet

        def term(n):
            return jnp.where(n < DRY, n - t, 0.0)

        east = jnp.where(lane == 127, DRY, roll(q, 127, 1))
        west = jnp.where(lane == 0, DRY, roll(q, 1, 1))
        inflow = (term(q_ref[k, 7:71, :]) + term(q_ref[k, 9:73, :])) + (term(west) + term(east))
        warm = t + mix_ref[k] * jnp.where(water, inflow, 0.0)
        feature = jnp.where(water, warm, 0.0)
        warm_ref[k] = warm
        fk_ref[pl.ds(k, 64, stride=16), :] = feature
        column = column + wet
        forcing = forcing + feature
    forcing = 0.01 * forcing
    fc_ref[0] = forcing
    fc_ref[1] = column

    copies[10].wait()
    copies[11].wait()
    level, lane16 = iota((24, 128), 0), iota((24, 128), 1)
    mx = jnp.zeros((24, 128), F32)
    for k in range(16):
        mx = jnp.where((level == k) | ((level == 16) & (lane16 == k)), mix_ref[k], mx)
    mx_ref[...] = mx

    def payload(r, first):
        own = jnp.concatenate([t_ref[:, r, :], wet_ref[:, r, :]], axis=0)
        feature = fk_ref[16 * r : 16 * r + 16, :]
        rows = [x[first : first + 8] for x in (forcing, column, np_ref[0], np_ref[1])]
        return own, jnp.concatenate([own, feature] + rows + [edge_pairs(t_ref, wet_ref, first)], axis=0)

    own_low, low = payload(0, 0)
    own_high, high = payload(63, 56)
    own_ref[...] = jnp.concatenate([own_low, own_high], axis=0)
    even = lat % 2 == 0
    pa_ref[...] = jnp.where(even, high, low)
    pb_ref[...] = jnp.where(even, low, high)

    @pl.when(lat == 7)
    def _():
        small = (8, 128)
        back = 127 - iota(small, 1)
        swap = iota(small, 1) ^ 1
        for i in range(11):
            x = high[8 * i : 8 * i + 8]
            x = lanes_from(x, swap if i == 10 else back)
            if i >= 6:
                x = jnp.concatenate([x[j : j + 1] for j in range(7, -1, -1)], axis=0)
            pb_ref[8 * i : 8 * i + 8, :] = x


def edge_pairs(t_ref, wet_ref, first):
    pair = iota((8, 128), 1) >> 1
    rt = jnp.zeros((8, 128), F32)
    for k in range(16):
        rt = jnp.where(pair == k, roll(t_ref[k, first : first + 8, :], 2 * k + 1, 1), rt)
        rt = jnp.where(pair == 16 + k, roll(wet_ref[k, first : first + 8, :], 33 + 2 * k, 1), rt)
    return rt


def edge_features(fk_ref, first):
    part = iota((8, 128), 1) >> 3
    rf = jnp.zeros((8, 128), F32)
    for k in range(16):
        rf = jnp.where(part == k, roll(fk_ref[pl.ds(16 * first + k, 8, stride=16), :], 8 * k + 4, 1), rf)
    return rf


def between(pa_ref, pb_ref, own_ref, fk_ref, fc_ref, rt_ref, rf_ref, np_ref, mx_ref,
            e4_ref, fb_ref, dd_ref, rfx_ref, qa_ref, qb_ref):
    lat = lax.axis_index("lat")
    even = lat % 2 == 0
    pa, pb = pa_ref[...], pb_ref[...]
    high = jnp.where(even, pa, pb)
    low = jnp.where(lat == 0, 0.0, jnp.where(even, pb, pa))
    level, lane16 = iota((16, 128), 0), iota((16, 128), 1)
    mix = mx_ref[0:16, :]

    def delta(halo, first):
        t, wet = own_ref[first : first + 16, :], own_ref[first + 16 : first + 32, :]
        return mix * (wet * halo[16:32]) * (halo[0:16] - t)

    d_low, d_high = delta(low, 0), delta(high, 32)
    dd_ref[0:16, :] = d_low
    dd_ref[16:32, :] = d_high
    f_out_low, f_low = low[32:48] - d_low, fk_ref[0:16, :] + d_low
    f_high, f_out_high = fk_ref[1008:1024, :] + d_high, high[32:48] - d_high
    fb_ref[...] = jnp.concatenate([f_out_low, f_low, f_high, f_out_high], axis=0)
    s_low = 0.01 * jnp.sum(d_low, axis=0, keepdims=True)
    s_high = 0.01 * jnp.sum(d_high, axis=0, keepdims=True)

    ext = (80, 128)
    lane, row = iota(ext, 1), iota(ext, 0)

    def extend(i, middle):
        first = 48 + 8 * i
        return jnp.concatenate([low[first : first + 8], middle, high[first : first + 8]], axis=0)

    forcing = extend(0, fc_ref[0])
    forcing = forcing + jnp.where(row == 8, s_low, 0.0) - jnp.where(row == 7, s_low, 0.0)
    forcing = forcing + jnp.where(row == 71, s_high, 0.0) - jnp.where(row == 72, s_high, 0.0)
    fields = [forcing, extend(1, fc_ref[1]), extend(2, np_ref[0]), extend(3, np_ref[1])]
    mixed = extend(4, rt_ref[...])
    for i, field in enumerate(fields):
        e4_ref[i] = field
        mixed = jnp.where(lane >> 4 == 4 + i, roll(field, 72 + 16 * i, 1), mixed)

    def laid(f):
        x = pltpu.roll(f, 4, 1, stride=8, stride_axis=0)
        return jnp.sum(jnp.where(lane16 >> 3 == level, x, 0.0), axis=0, keepdims=True)

    zero = jnp.zeros((8, 128), F32)
    rf = jnp.concatenate([zero, rf_ref[...], zero], axis=0)
    for at, f in ((7, f_out_low), (8, f_low), (71, f_high), (72, f_out_high)):
        rf = jnp.where(row == at, laid(f), rf)
    rfx_ref[...] = rf

    small = iota((8, 128), 1)

    def columns(side):
        wide = 64 + 16 * ((small - 64) >> 3) + 8 * side + (small & 7)
        index = jnp.where(small < 32, 2 * small + side, jnp.where(small < 64, 0, wide))
        index_f = jnp.where((small >= 32) & (small < 48), 8 * (small - 32) + 3 + side, 0)
        parts = []
        for i in range(10):
            a = lanes_from(mixed[8 * i : 8 * i + 8], index)
            b = lanes_from(rf[8 * i : 8 * i + 8], index_f)
            parts.append(jnp.where((small >= 32) & (small < 48), b, a))
        return jnp.concatenate(parts, axis=0)

    first_core = lax.axis_index("lon") % 2 == 0
    q_east, q_west = columns(0), columns(1)
    qa_ref[...] = jnp.where(first_core, q_east, q_west)
    qb_ref[...] = jnp.where(first_core, q_west, q_east)


def layers(w1, w2, w3, window):
    h = gelu_twice(jnp.dot(w1, window, preferred_element_type=F32)).astype(BF16)
    y = gelu_twice(jnp.dot(w2, h, preferred_element_type=F32)).astype(BF16)
    net = jnp.dot(w3, y, preferred_element_type=F32)
    return 0.5 * net.astype(BF16).astype(F32)


def put(planes, at, x):
    n = x.shape[0]
    for plane, shift in zip(planes, (1, 0, 127)):
        plane[at : at + n, :] = roll(x, shift, 1).astype(BF16)


def chunk(weights, planes, starts, g_ref, at):
    w1, w2, w3 = (w[...] for w in weights)
    windows = [jnp.concatenate([f[16 * r : 16 * r + 48, :] for f in planes], axis=0) for r in starts]
    net = layers(w1, w2, w3, jnp.concatenate(windows, axis=1))
    for i in range(16):
        g_ref[16 * (at + i) : 16 * (at + i) + 16, :] = net[:, 128 * i : 128 * i + 128]


def inner_chunk(fk_ref, weights, planes, c, g_ref, at):
    put(planes, 0, fk_ref[16 * (7 + 16 * c) : 16 * (25 + 16 * c), :])
    chunk(weights, planes, range(16), g_ref, at)


def early_rows():
    lon, lat = lax.axis_index("lon"), lax.axis_index("lat")
    place = (lon % 16) // 2
    return (lat == 7) & (place <= 2), (lat == 7) & (place <= 1)


def late_rows():
    return lax.axis_index("lon") % 16 >= 14


def ahead(fk_ref, w1_ref, w2_ref, w3_ref, w1_out, w2_out, w3_out, g_ref, *planes):
    w1_out[...] = jnp.concatenate([w1_ref[3 * a + b] for b in range(3) for a in range(3)], axis=1)
    w2_out[...] = (w2_ref[...].astype(F32) * 0.5).astype(BF16)
    w3_out[...] = (w3_ref[...].astype(F32) * 0.5).astype(BF16)
    weights = (w1_out, w2_out, w3_out)
    for c, early in enumerate(early_rows()):
        pl.when(early)(functools.partial(inner_chunk, fk_ref, weights, planes, c, g_ref, 16 * c))


def middle_rows(fk_ref, t_ref, wet_ref, w1_ref, w2_ref, w3_ref, done_ref, g_ref, rt_ref, rf_ref, *planes):
    weights = (w1_ref, w2_ref, w3_ref)
    for c, early in enumerate(early_rows()):
        skip = early | late_rows() if c else early
        pl.when(jnp.logical_not(skip))(functools.partial(inner_chunk, fk_ref, weights, planes, c, g_ref, 16 * c))

        def take(c=c):
            g_ref[256 * c : 256 * c + 256, :] = done_ref[256 * c : 256 * c + 256, :]

        pl.when(early)(take)
    for i in range(0, 64, 8):
        rt_ref[i : i + 8, :] = edge_pairs(t_ref, wet_ref, i)
        rf_ref[i : i + 8, :] = edge_features(fk_ref, i)
    inner_chunk(fk_ref, weights, planes, 2, g_ref, 32)


def outer_rows(fk_ref, fb_ref, w1_ref, w2_ref, w3_ref, g1_ref, g_ref, *planes):
    weights = (w1_ref, w2_ref, w3_ref)
    late = late_rows()
    pl.when(late)(functools.partial(inner_chunk, fk_ref, weights, planes, 1, g_ref, 16))

    @pl.when(jnp.logical_not(late))
    def _():
        g_ref[256:512, :] = g1_ref[256:512, :]

    put(planes, 0, fb_ref[0:32, :])
    put(planes, 16 * 2, fk_ref[16 : 16 * 9, :])
    put(planes, 16 * 10, fk_ref[16 * 55 : 16 * 63, :])
    put(planes, 16 * 18, fb_ref[32:64, :])
    chunk(weights, planes, [r + 2 * (r >= 8) for r in range(16)], g_ref, 0)


def closing(qa_ref, qb_ref, ha_ref, hb_ref, rf_ref, e4_ref, dd_ref, warm_ref, wet_ref,
            g1_ref, g2_ref, w1_ref, w2_ref, w3_ref, mx_ref, out_hbm, eta_hbm, mid_hbm, out_ref, eta_ref, sems):
    first_core = lax.axis_index("lon") % 2 == 0
    ext = (80, 128)
    lane = iota(ext, 1)
    small, sub = iota((8, 128), 1), iota((8, 128), 0)
    qa, qb, ha, hb = qa_ref[...], qb_ref[...], ha_ref[...], hb_ref[...]
    q_west, q_east = jnp.where(first_core, qb, qa), jnp.where(first_core, qa, qb)
    h_west, h_east = jnp.where(first_core, hb, ha), jnp.where(first_core, ha, hb)
    mix = mx_ref[16:17, :]

    def delta(halo, own):
        return mix * roll(halo * own, 112, 1) * (halo - own)

    d_west, d_east = delta(h_west, q_west), delta(h_east, q_east)

    rf = rf_ref[...]
    index_w = jnp.where(small < 64, 8 * (small & 15) + 3 + (small >> 4), 0)
    index_e = jnp.where(small < 64, 8 * (small & 15) + 1 + (small >> 4), 0)
    f_west = jnp.concatenate([lanes_from(rf[8 * i : 8 * i + 8], index_w) for i in range(10)], axis=0)
    f_east = jnp.concatenate([lanes_from(rf[8 * i : 8 * i + 8], index_e) for i in range(10)], axis=0)
    which = lane >> 4
    f_west = jnp.where(which == 0, roll(h_west, 96, 1) - d_west,
                       f_west + jnp.where(which == 1, roll(d_west, 16, 1), 0.0))
    f_east = jnp.where(which == 3, roll(h_east, 16, 1) - roll(d_east, 48, 1),
                       f_east + jnp.where(which == 2, roll(d_east, 32, 1), 0.0))
    cells = [f_east, roll(f_east, 112, 1), f_west, roll(f_west, 112, 1)]
    blank = jnp.zeros((128, 80), BF16)
    x = jnp.zeros((256, 128), F32)
    for a in range(3):
        window = jnp.concatenate([c[7 + a : 71 + a] for c in cells], axis=0).astype(BF16)
        w = jnp.concatenate([w1_ref[3 * a + b] for b in range(3)] + [blank], axis=1)
        x = x + lax.dot_general(window, w, NT, preferred_element_type=F32)

    side = []
    for i in range(4):
        east = roll(h_east, 128 - (64 + 8 * i), 1)
        west = roll(h_west, 56 - 8 * i, 1)
        side.append(jnp.where(lane < 8, east, jnp.where(lane >= 120, west, 0.0)))
    main = [e4_ref[i] for i in range(4)]
    s_west = 0.01 * jnp.sum(d_west, axis=1, keepdims=True)
    s_east = 0.01 * jnp.sum(d_east, axis=1, keepdims=True)
    push = [main[0] + jnp.where(lane == 0, s_west, 0.0) + jnp.where(lane == 127, s_east, 0.0),
            side[0] - jnp.where(lane == 127, s_west, 0.0) - jnp.where(lane == 0, s_east, 0.0)]
    speed = [0.45 * x / 16 for x in (main[1], side[1])]

    def neighbours(pair):
        out = []
        for i in range(2):
            x, other = pair[i], pair[1 - i]
            out.append((roll(jnp.where(lane == 0, other, x), 127, 1),
                        roll(jnp.where(lane == 127, other, x), 1, 1),
                        roll(x, 79, 0), roll(x, 1, 0)))
        return out

    active = [jnp.where(s > 0.0, 1.0, 0.0).astype(F32) for s in speed]
    facing = [[jnp.minimum(s, n) for n in ns] for s, ns in zip(speed, neighbours(speed))]

    def advance(current, earlier):
        fresh = []
        for i, ns in enumerate(neighbours(current)):
            c = current[i]
            change = 2.0 * c - earlier[i] + push[i]
            for f, n in zip(facing[i], ns):
                change = change + f * (n - c)
            fresh.append(active[i] * change)
        return fresh, current

    state = ([main[2], side[2]], [main[3], side[3]])

    h = gelu_twice(x).astype(BF16)
    x = lax.dot_general(h, w2_ref[...], NT, preferred_element_type=F32)
    state = advance(*state)
    state = advance(*state)
    y = gelu_twice(x).astype(BF16)
    w3 = jnp.concatenate([w3_ref[...], jnp.zeros((112, 512), BF16)], axis=0)
    net = lax.dot_general(y, w3, NT, preferred_element_type=F32)
    for _ in range(SUB - 2):
        state = advance(*state)
    eta_ref[0] = state[0][0][8:72]
    eta_ref[1] = state[1][0][8:72]
    copies = [pltpu.make_async_copy(eta_ref.at[0], eta_hbm, sems.at[4]),
              pltpu.make_async_copy(eta_ref.at[1], mid_hbm, sems.at[5])]
    copies[0].start()
    copies[1].start()

    net = 0.5 * net.astype(BF16).astype(F32)
    ends = [net[64 * c : 64 * c + 64] for c in range(4)]
    low16 = lane[:64] < 16
    ends[1] = ends[1] + jnp.where(low16, d_east[8:72], 0.0)
    ends[2] = ends[2] + jnp.where(low16, d_west[8:72], 0.0)
    spread = jnp.where(small < 64, small >> 2, 0)
    edges = []
    for i in range(8):
        x = jnp.zeros((8, 128), F32)
        for c in range(4):
            x = jnp.where(small & 3 == c, lanes_from(ends[c][8 * i : 8 * i + 8], spread), x)
        edges.append(x)

    at_edge = (small < 2) | (small >= 126)
    for k in range(16):
        for i in range(8):
            if i == 0 or i == 7:
                g = g2_ref[pl.ds((0 if i == 0 else 128) + k, 8, stride=16), :]
            elif i == 3 or i == 4:
                g = g2_ref[pl.ds((8 * i - 8) * 16 + k, 8, stride=16), :]
            else:
                g = g1_ref[pl.ds((8 * i - 8) * 16 + k, 8, stride=16), :]
            g = jnp.where(at_edge, roll(edges[i], 126 - 4 * k, 1), g)
            y = warm_ref[k, 8 * i : 8 * i + 8, :] + wet_ref[k, 8 * i : 8 * i + 8, :] * g
            if i == 0:
                y = y + jnp.where(sub == 0, dd_ref[k : k + 1, :], 0.0)
            if i == 7:
                y = y + jnp.where(sub == 7, dd_ref[16 + k : 17 + k, :], 0.0)
            out_ref[k, 8 * i : 8 * i + 8, :] = y
        if k % 4 == 3:
            part = pl.ds(k - 3, 4)
            copies.append(pltpu.make_async_copy(out_ref.at[part], out_hbm.at[part], sems.at[k // 4]))
            copies[-1].start()
    for copy in copies:
        copy.wait()


def partners(partner):
    pairs = []
    for lon in range(32):
        for lat in range(8):
            to = partner(lon, lat)
            pairs.append((8 * lon + lat, 8 * (to[0] % 32) + to[1]))
    return pairs


LAT_A = partners(lambda lon, lat: (lon, lat ^ 1))
LAT_B = partners(
    lambda lon, lat: (31 - lon, 7) if lat == 7 else (lon ^ 1, 0) if lat == 0 else (lon, lat + 1 if lat % 2 else lat - 1)
)
LON_A = partners(lambda lon, lat: (lon ^ 1, lat))
LON_B = partners(lambda lon, lat: (lon + 1 if lon % 2 else lon - 1, lat))


def swap(x, pairs):
    return lax.ppermute(x, ("lon", "lat"), pairs)


def on_device(t, now, prior, liquid, depth, mix, w1, w2, w3):
    cube, flat, tall, inner = (16, 64, 128), (64, 128), (80, 128), (768, 128)
    tv, warm, wet, fk, fc, own, both, mx, pa, pb = call(
        inside,
        (shape(*cube), shape(*cube), shape(*cube), shape(1024, 128), shape(2, 64, 128),
         shape(*flat), shape(2, 64, 128), shape(24, 128), shape(88, 128), shape(88, 128)),
        scratch=(pltpu.VMEM(cube, jnp.int32), pltpu.VMEM(flat, jnp.int32), pltpu.SMEM((16,), F32),
                 pltpu.VMEM((16, 80, 128), F32), pltpu.SemaphoreType.DMA((12,))),
        specs=[HB] * 6, name="inside", flops=10**7, moved=2 * 10**6,
    )(*(pltpu.with_memory_space_constraint(x, pltpu.HBM) for x in (t, liquid, depth, now, prior, mix)))
    planes = [pltpu.VMEM((20 * 16, 128), BF16)] * 3
    ra = swap(pa, LAT_A)
    v1, v2, v3, gp = call(
        ahead, (shape(128, 144, dtype=BF16), shape(512, 128, dtype=BF16), shape(16, 512, dtype=BF16), shape(512, 128)),
        scratch=planes, specs=[VM] * 4, name="ahead", flops=10**6, moved=10**5,
    )(fk, w1, w2, w3)
    pb, gp = lax.optimization_barrier((pb, gp))
    rb = swap(pb, LAT_B)
    g1, rt, rf = call(middle_rows, (shape(*inner), shape(*flat), shape(*flat)), scratch=planes,
                      specs=[VM] * 7, name="middle_rows", flops=10**9, moved=10**6,
                      )(fk, tv, wet, v1, v2, v3, gp)
    e4, fb, dd, rfx, qa, qb = call(
        between,
        (shape(4, 80, 128), shape(64, 128), shape(32, 128), shape(*tall), shape(*tall), shape(*tall)),
        specs=[VM] * 9, name="between", flops=10**7, moved=10**6,
    )(ra, rb, own, fk, fc, rt, rf, both, mx)
    hb = swap(qb, LON_B)
    ha = swap(qa, LON_A)
    g2 = call(outer_rows, shape(512, 128), scratch=planes, specs=[VM] * 6, name="outer_rows",
              flops=5 * 10**8, moved=10**6)(fk, fb, v1, v2, v3, g1)
    return call(
        closing,
        (shape(*cube), shape(*flat), shape(*flat)),
        scratch=(pltpu.VMEM(cube, F32), pltpu.VMEM((2, 64, 128), F32), pltpu.SemaphoreType.DMA((6,))),
        specs=[VM] * 15, out_specs=(HB, HB, HB), name="closing", flops=10**8, moved=3 * 10**6,
    )(qa, qb, ha, hb, rfx, e4, dd, warm, wet, g1, g2, w1, v2, v3, mx)


def solution(mesh):
    wide, flat = P(None, "lat", "lon"), P("lat", "lon")
    return jax.shard_map(
        on_device,
        mesh=mesh,
        in_specs=(wide, flat, flat, wide, flat, P(), P(), P(), P()),
        out_specs=(wide, flat, flat),
        check_vma=False,
    )
```

```python
import functools

import jax
import jax.numpy as jnp
from jax import lax
from jax.experimental import pallas as pl
from jax.experimental.pallas import tpu as pltpu
from jax.sharding import PartitionSpec as P

SUB = 8
F32 = jnp.float32
BF16 = jnp.bfloat16
C0 = 0.7978845608028654
C1 = 0.044715 * C0
DRY = 1e30
VM = pl.BlockSpec(memory_space=pltpu.VMEM)
HB = pl.BlockSpec(memory_space=pltpu.HBM)
NT = (((1,), (1,)), ((), ()))


def iota(shape, axis):
    return lax.broadcasted_iota(jnp.int32, shape, axis)


def roll(x, shift, axis):
    size = x.shape[axis]
    shift = shift % size
    return x if shift == 0 else pltpu.roll(x, shift, axis)


def lanes_from(x, index):
    return jnp.take_along_axis(x, index, axis=1)


def gelu_twice(x):
    return x + x * jnp.tanh(x * (C0 + C1 * (x * x)))


def call(body, outs, scratch=(), specs=None, out_specs=None, flops=0, moved=0, room=40, **given):
    return pl.pallas_call(
        body,
        out_shape=outs,
        in_specs=specs,
        out_specs=out_specs or jax.tree.map(lambda _: VM, outs),
        scratch_shapes=list(scratch),
        compiler_params=pltpu.CompilerParams(vmem_limit_bytes=room * 1024 * 1024),
        cost_estimate=pl.CostEstimate(flops=flops, bytes_accessed=moved, transcendentals=0),
        **given,
    )


def shape(*dims, dtype=F32):
    return jax.ShapeDtypeStruct(dims, dtype)


def inside(t_hbm, l_hbm, d_hbm, now_hbm, prior_hbm, mix_hbm,
           t_ref, warm_ref, wet_ref, fk_ref, fc_ref, own_ref, np_ref, mx_ref, pa_ref, pb_ref,
           l_ref, d_ref, mix_ref, q_ref, sems):
    lat = lax.axis_index("lat")
    copies = [pltpu.make_async_copy(d_hbm, d_ref, sems.at[0]), pltpu.make_async_copy(mix_hbm, mix_ref, sems.at[1])]
    for c in range(4):
        part = pl.ds(4 * c, 4)
        copies.append(pltpu.make_async_copy(t_hbm.at[part], t_ref.at[part], sems.at[2 + 2 * c]))
        copies.append(pltpu.make_async_copy(l_hbm.at[part], l_ref.at[part], sems.at[3 + 2 * c]))
    copies.append(pltpu.make_async_copy(now_hbm, np_ref.at[0], sems.at[10]))
    copies.append(pltpu.make_async_copy(prior_hbm, np_ref.at[1], sems.at[11]))
    for copy in copies:
        copy.start()
    dims = (64, 128)
    lane = iota(dims, 1)
    q_ref[:, 0:8, :] = jnp.full((16, 8, 128), DRY, F32)
    q_ref[:, 72:80, :] = jnp.full((16, 8, 128), DRY, F32)
    column = jnp.zeros(dims, F32)
    forcing = jnp.zeros(dims, F32)
    copies[0].wait()
    copies[1].wait()
    depth = d_ref[...]
    for k in range(16):
        if k % 4 == 0:
            copies[2 + k // 2].wait()
            copies[3 + k // 2].wait()
        t = t_ref[k]
        water = (l_ref[k] > 0) & (k < depth)
        q = jnp.where(water, t, DRY)
        q_ref[k, 8:72, :] = q
        wet = jnp.where(water, 1.0, 0.0).astype(F32)
        wet_ref[k] = wet

        def term(n):
            return jnp.where(n < DRY, n - t, 0.0)

        east = jnp.where(lane == 127, DRY, roll(q, 127, 1))
        west = jnp.where(lane == 0, DRY, roll(q, 1, 1))
        inflow = (term(q_ref[k, 7:71, :]) + term(q_ref[k, 9:73, :])) + (term(west) + term(east))
        warm = t + mix_ref[k] * jnp.where(water, inflow, 0.0)
        feature = jnp.where(water, warm, 0.0)
        warm_ref[k] = warm
        fk_ref[pl.ds(k, 64, stride=16), :] = feature
        column = column + wet
        forcing = forcing + feature
    forcing = 0.01 * forcing
    fc_ref[0] = forcing
    fc_ref[1] = column

    copies[10].wait()
    copies[11].wait()
    level, lane16 = iota((24, 128), 0), iota((24, 128), 1)
    mx = jnp.zeros((24, 128), F32)
    for k in range(16):
        mx = jnp.where((level == k) | ((level == 16) & (lane16 == k)), mix_ref[k], mx)
    mx_ref[...] = mx

    def payload(r, first):
        own = jnp.concatenate([t_ref[:, r, :], wet_ref[:, r, :]], axis=0)
        feature = fk_ref[16 * r : 16 * r + 16, :]
        rows = [x[first : first + 8] for x in (forcing, column, np_ref[0], np_ref[1])]
        return own, jnp.concatenate([own, feature] + rows + [edge_pairs(t_ref, wet_ref, first)], axis=0)

    own_low, low = payload(0, 0)
    own_high, high = payload(63, 56)
    own_ref[...] = jnp.concatenate([own_low, own_high], axis=0)
    even = lat % 2 == 0
    pa_ref[...] = jnp.where(even, high, low)
    pb_ref[...] = jnp.where(even, low, high)

    @pl.when(lat == 7)
    def _():
        small = (8, 128)
        back = 127 - iota(small, 1)
        swap = iota(small, 1) ^ 1
        for i in range(11):
            x = high[8 * i : 8 * i + 8]
            x = lanes_from(x, swap if i == 10 else back)
            if i >= 6:
                x = jnp.concatenate([x[j : j + 1] for j in range(7, -1, -1)], axis=0)
            pb_ref[8 * i : 8 * i + 8, :] = x


def edge_pairs(t_ref, wet_ref, first):
    pair = iota((8, 128), 1) >> 1
    rt = jnp.zeros((8, 128), F32)
    for k in range(16):
        rt = jnp.where(pair == k, roll(t_ref[k, first : first + 8, :], 2 * k + 1, 1), rt)
        rt = jnp.where(pair == 16 + k, roll(wet_ref[k, first : first + 8, :], 33 + 2 * k, 1), rt)
    return rt


def edge_features(fk_ref, first):
    part = iota((8, 128), 1) >> 3
    rf = jnp.zeros((8, 128), F32)
    for k in range(16):
        rf = jnp.where(part == k, roll(fk_ref[pl.ds(16 * first + k, 8, stride=16), :], 8 * k + 4, 1), rf)
    return rf


def between(pa_ref, pb_ref, own_ref, fk_ref, fc_ref, rt_ref, rf_ref, np_ref, mx_ref,
            e4_ref, fb_ref, dd_ref, rfx_ref, qa_ref, qb_ref):
    lat = lax.axis_index("lat")
    even = lat % 2 == 0
    pa, pb = pa_ref[...], pb_ref[...]
    high = jnp.where(even, pa, pb)
    low = jnp.where(lat == 0, 0.0, jnp.where(even, pb, pa))
    level, lane16 = iota((16, 128), 0), iota((16, 128), 1)
    mix = mx_ref[0:16, :]

    def delta(halo, first):
        t, wet = own_ref[first : first + 16, :], own_ref[first + 16 : first + 32, :]
        return mix * (wet * halo[16:32]) * (halo[0:16] - t)

    d_low, d_high = delta(low, 0), delta(high, 32)
    dd_ref[0:16, :] = d_low
    dd_ref[16:32, :] = d_high
    f_out_low, f_low = low[32:48] - d_low, fk_ref[0:16, :] + d_low
    f_high, f_out_high = fk_ref[1008:1024, :] + d_high, high[32:48] - d_high
    fb_ref[...] = jnp.concatenate([f_out_low, f_low, f_high, f_out_high], axis=0)
    s_low = 0.01 * jnp.sum(d_low, axis=0, keepdims=True)
    s_high = 0.01 * jnp.sum(d_high, axis=0, keepdims=True)

    ext = (80, 128)
    lane, row = iota(ext, 1), iota(ext, 0)

    def extend(i, middle):
        first = 48 + 8 * i
        return jnp.concatenate([low[first : first + 8], middle, high[first : first + 8]], axis=0)

    forcing = extend(0, fc_ref[0])
    forcing = forcing + jnp.where(row == 8, s_low, 0.0) - jnp.where(row == 7, s_low, 0.0)
    forcing = forcing + jnp.where(row == 71, s_high, 0.0) - jnp.where(row == 72, s_high, 0.0)
    fields = [forcing, extend(1, fc_ref[1]), extend(2, np_ref[0]), extend(3, np_ref[1])]
    mixed = extend(4, rt_ref[...])
    for i, field in enumerate(fields):
        e4_ref[i] = field
        mixed = jnp.where(lane >> 4 == 4 + i, roll(field, 72 + 16 * i, 1), mixed)

    def laid(f):
        x = pltpu.roll(f, 4, 1, stride=8, stride_axis=0)
        return jnp.sum(jnp.where(lane16 >> 3 == level, x, 0.0), axis=0, keepdims=True)

    zero = jnp.zeros((8, 128), F32)
    rf = jnp.concatenate([zero, rf_ref[...], zero], axis=0)
    for at, f in ((7, f_out_low), (8, f_low), (71, f_high), (72, f_out_high)):
        rf = jnp.where(row == at, laid(f), rf)
    rfx_ref[...] = rf

    small = iota((8, 128), 1)

    def columns(side):
        wide = 64 + 16 * ((small - 64) >> 3) + 8 * side + (small & 7)
        index = jnp.where(small < 32, 2 * small + side, jnp.where(small < 64, 0, wide))
        index_f = jnp.where((small >= 32) & (small < 48), 8 * (small - 32) + 3 + side, 0)
        parts = []
        for i in range(10):
            a = lanes_from(mixed[8 * i : 8 * i + 8], index)
            b = lanes_from(rf[8 * i : 8 * i + 8], index_f)
            parts.append(jnp.where((small >= 32) & (small < 48), b, a))
        return jnp.concatenate(parts, axis=0)

    first_core = lax.axis_index("lon") % 2 == 0
    q_east, q_west = columns(0), columns(1)
    qa_ref[...] = jnp.where(first_core, q_east, q_west)
    qb_ref[0:80, :] = jnp.where(first_core, q_west, q_east)
    qb_ref[80:96, :] = jnp.zeros((16, 128), F32)


def layers(w1, w2, w3, window):
    h = gelu_twice(jnp.dot(w1, window, preferred_element_type=F32)).astype(BF16)
    y = gelu_twice(jnp.dot(w2, h, preferred_element_type=F32)).astype(BF16)
    net = jnp.dot(w3, y, preferred_element_type=F32)
    return 0.5 * net.astype(BF16).astype(F32)


def put(planes, at, x):
    n = x.shape[0]
    for plane, shift in zip(planes, (1, 0, 127)):
        plane[at : at + n, :] = roll(x, shift, 1).astype(BF16)


def chunk(weights, planes, starts, g_ref, at):
    w1, w2, w3 = (w[...] for w in weights)
    windows = [jnp.concatenate([f[16 * r : 16 * r + 48, :] for f in planes], axis=0) for r in starts]
    net = layers(w1, w2, w3, jnp.concatenate(windows, axis=1))
    for i in range(16):
        g_ref[16 * (at + i) : 16 * (at + i) + 16, :] = net[:, 128 * i : 128 * i + 128]


def inner_chunk(fk_ref, weights, planes, c, g_ref, at):
    put(planes, 0, fk_ref[16 * (7 + 16 * c) : 16 * (25 + 16 * c), :])
    chunk(weights, planes, range(16), g_ref, at)


def early_rows():
    lon, lat = lax.axis_index("lon"), lax.axis_index("lat")
    place = (lon % 16) // 2
    return (lat == 7) & (place <= 2)


def late_rows():
    return lax.axis_index("lon") % 16 >= 14


def ahead(fk_ref, w1_ref, w2_ref, w3_ref, w1_out, w2_out, w3_out, g_ref, *planes):
    w1_out[...] = jnp.concatenate([w1_ref[3 * a + b] for b in range(3) for a in range(3)], axis=1)
    w2_out[...] = (w2_ref[...].astype(F32) * 0.5).astype(BF16)
    w3_out[...] = (w3_ref[...].astype(F32) * 0.5).astype(BF16)
    weights = (w1_out, w2_out, w3_out)
    pl.when(early_rows())(functools.partial(inner_chunk, fk_ref, weights, planes, 0, g_ref, 0))


def middle_rows(fk_ref, t_ref, wet_ref, w1_ref, w2_ref, w3_ref, done_ref, g_ref, rt_ref, rf_ref, *planes):
    weights = (w1_ref, w2_ref, w3_ref)
    early = early_rows()
    pl.when(jnp.logical_not(early))(functools.partial(inner_chunk, fk_ref, weights, planes, 0, g_ref, 0))

    @pl.when(early)
    def _():
        g_ref[0:256, :] = done_ref[...]

    pl.when(jnp.logical_not(late_rows()))(functools.partial(inner_chunk, fk_ref, weights, planes, 1, g_ref, 16))
    for i in range(0, 64, 8):
        rt_ref[i : i + 8, :] = edge_pairs(t_ref, wet_ref, i)
        rf_ref[i : i + 8, :] = edge_features(fk_ref, i)
    inner_chunk(fk_ref, weights, planes, 2, g_ref, 32)


def outer_rows(fk_ref, fb_ref, w1_ref, w2_ref, w3_ref, g1_ref, g_ref, *planes):
    weights = (w1_ref, w2_ref, w3_ref)
    late = late_rows()
    pl.when(late)(functools.partial(inner_chunk, fk_ref, weights, planes, 1, g_ref, 16))

    @pl.when(jnp.logical_not(late))
    def _():
        g_ref[256:512, :] = g1_ref[256:512, :]

    put(planes, 0, fb_ref[0:32, :])
    put(planes, 16 * 2, fk_ref[16 : 16 * 9, :])
    put(planes, 16 * 10, fk_ref[16 * 55 : 16 * 63, :])
    put(planes, 16 * 18, fb_ref[32:64, :])
    chunk(weights, planes, [r + 2 * (r >= 8) for r in range(16)], g_ref, 0)


def closing(qa_ref, qb_ref, ha_ref, hb_ref, rf_ref, e4_ref, dd_ref, warm_ref, wet_ref,
            g1_ref, g2_ref, w1_ref, w2_ref, w3_ref, mx_ref, out_hbm, eta_hbm, mid_hbm, out_ref, eta_ref, sems):
    first_core = lax.axis_index("lon") % 2 == 0
    ext = (80, 128)
    lane = iota(ext, 1)
    small, sub = iota((8, 128), 1), iota((8, 128), 0)
    qa, qb, ha, hb = qa_ref[...], qb_ref[0:80, :], ha_ref[...], hb_ref[0:80, :]
    q_west, q_east = jnp.where(first_core, qb, qa), jnp.where(first_core, qa, qb)
    h_west, h_east = jnp.where(first_core, hb, ha), jnp.where(first_core, ha, hb)
    mix = mx_ref[16:17, :]

    def delta(halo, own):
        return mix * roll(halo * own, 112, 1) * (halo - own)

    d_west, d_east = delta(h_west, q_west), delta(h_east, q_east)

    rf = rf_ref[...]
    index_w = jnp.where(small < 64, 8 * (small & 15) + 3 + (small >> 4), 0)
    index_e = jnp.where(small < 64, 8 * (small & 15) + 1 + (small >> 4), 0)
    f_west = jnp.concatenate([lanes_from(rf[8 * i : 8 * i + 8], index_w) for i in range(10)], axis=0)
    f_east = jnp.concatenate([lanes_from(rf[8 * i : 8 * i + 8], index_e) for i in range(10)], axis=0)
    which = lane >> 4
    f_west = jnp.where(which == 0, roll(h_west, 96, 1) - d_west,
                       f_west + jnp.where(which == 1, roll(d_west, 16, 1), 0.0))
    f_east = jnp.where(which == 3, roll(h_east, 16, 1) - roll(d_east, 48, 1),
                       f_east + jnp.where(which == 2, roll(d_east, 32, 1), 0.0))
    cells = [f_east, roll(f_east, 112, 1), f_west, roll(f_west, 112, 1)]
    blank = jnp.zeros((128, 80), BF16)
    x = jnp.zeros((256, 128), F32)
    for a in range(3):
        window = jnp.concatenate([c[7 + a : 71 + a] for c in cells], axis=0).astype(BF16)
        w = jnp.concatenate([w1_ref[3 * a + b] for b in range(3)] + [blank], axis=1)
        x = x + lax.dot_general(window, w, NT, preferred_element_type=F32)

    side = []
    for i in range(4):
        east = roll(h_east, 128 - (64 + 8 * i), 1)
        west = roll(h_west, 56 - 8 * i, 1)
        side.append(jnp.where(lane < 8, east, jnp.where(lane >= 120, west, 0.0)))
    main = [e4_ref[i] for i in range(4)]
    s_west = 0.01 * jnp.sum(d_west, axis=1, keepdims=True)
    s_east = 0.01 * jnp.sum(d_east, axis=1, keepdims=True)
    push = [main[0] + jnp.where(lane == 0, s_west, 0.0) + jnp.where(lane == 127, s_east, 0.0),
            side[0] - jnp.where(lane == 127, s_west, 0.0) - jnp.where(lane == 0, s_east, 0.0)]
    speed = [0.45 * x / 16 for x in (main[1], side[1])]

    def neighbours(pair):
        out = []
        for i in range(2):
            x, other = pair[i], pair[1 - i]
            out.append((roll(jnp.where(lane == 0, other, x), 127, 1),
                        roll(jnp.where(lane == 127, other, x), 1, 1),
                        roll(x, 79, 0), roll(x, 1, 0)))
        return out

    active = [jnp.where(s > 0.0, 1.0, 0.0).astype(F32) for s in speed]
    facing = [[jnp.minimum(s, n) for n in ns] for s, ns in zip(speed, neighbours(speed))]

    def advance(current, earlier):
        fresh = []
        for i, ns in enumerate(neighbours(current)):
            c = current[i]
            change = 2.0 * c - earlier[i] + push[i]
            for f, n in zip(facing[i], ns):
                change = change + f * (n - c)
            fresh.append(active[i] * change)
        return fresh, current

    state = ([main[2], side[2]], [main[3], side[3]])

    h = gelu_twice(x).astype(BF16)
    x = lax.dot_general(h, w2_ref[...], NT, preferred_element_type=F32)
    state = advance(*state)
    state = advance(*state)
    y = gelu_twice(x).astype(BF16)
    w3 = jnp.concatenate([w3_ref[...], jnp.zeros((112, 512), BF16)], axis=0)
    net = lax.dot_general(y, w3, NT, preferred_element_type=F32)
    for _ in range(SUB - 2):
        state = advance(*state)
    eta_ref[0] = state[0][0][8:72]
    eta_ref[1] = state[1][0][8:72]
    copies = [pltpu.make_async_copy(eta_ref.at[0], eta_hbm, sems.at[4]),
              pltpu.make_async_copy(eta_ref.at[1], mid_hbm, sems.at[5])]
    copies[0].start()
    copies[1].start()

    net = 0.5 * net.astype(BF16).astype(F32)
    ends = [net[64 * c : 64 * c + 64] for c in range(4)]
    low16 = lane[:64] < 16
    ends[1] = ends[1] + jnp.where(low16, d_east[8:72], 0.0)
    ends[2] = ends[2] + jnp.where(low16, d_west[8:72], 0.0)
    spread = jnp.where(small < 64, small >> 2, 0)
    edges = []
    for i in range(8):
        x = jnp.zeros((8, 128), F32)
        for c in range(4):
            x = jnp.where(small & 3 == c, lanes_from(ends[c][8 * i : 8 * i + 8], spread), x)
        edges.append(x)

    at_edge = (small < 2) | (small >= 126)
    for k in range(16):
        for i in range(8):
            if i == 0 or i == 7:
                g = g2_ref[pl.ds((0 if i == 0 else 128) + k, 8, stride=16), :]
            elif i == 3 or i == 4:
                g = g2_ref[pl.ds((8 * i - 8) * 16 + k, 8, stride=16), :]
            else:
                g = g1_ref[pl.ds((8 * i - 8) * 16 + k, 8, stride=16), :]
            g = jnp.where(at_edge, roll(edges[i], 126 - 4 * k, 1), g)
            y = warm_ref[k, 8 * i : 8 * i + 8, :] + wet_ref[k, 8 * i : 8 * i + 8, :] * g
            if i == 0:
                y = y + jnp.where(sub == 0, dd_ref[k : k + 1, :], 0.0)
            if i == 7:
                y = y + jnp.where(sub == 7, dd_ref[16 + k : 17 + k, :], 0.0)
            out_ref[k, 8 * i : 8 * i + 8, :] = y
        if k % 4 == 3:
            part = pl.ds(k - 3, 4)
            copies.append(pltpu.make_async_copy(out_ref.at[part], out_hbm.at[part], sems.at[k // 4]))
            copies[-1].start()
    for copy in copies:
        copy.wait()


def partners(partner):
    pairs = []
    for lon in range(32):
        for lat in range(8):
            to = partner(lon, lat)
            pairs.append((8 * lon + lat, 8 * (to[0] % 32) + to[1]))
    return pairs


LAT_A = partners(lambda lon, lat: (lon, lat ^ 1))
LAT_B = partners(
    lambda lon, lat: (31 - lon, 7) if lat == 7 else (lon ^ 1, 0) if lat == 0 else (lon, lat + 1 if lat % 2 else lat - 1)
)
LON_A = partners(lambda lon, lat: (lon ^ 1, lat))
LON_B = partners(lambda lon, lat: (lon + 1 if lon % 2 else lon - 1, lat))


def swap(x, pairs):
    return lax.ppermute(x, ("lon", "lat"), pairs)


def on_device(t, now, prior, liquid, depth, mix, w1, w2, w3):
    cube, flat, tall, inner = (16, 64, 128), (64, 128), (80, 128), (768, 128)
    tv, warm, wet, fk, fc, own, both, mx, pa, pb = call(
        inside,
        (shape(*cube), shape(*cube), shape(*cube), shape(1024, 128), shape(2, 64, 128),
         shape(*flat), shape(2, 64, 128), shape(24, 128), shape(88, 128), shape(88, 128)),
        scratch=(pltpu.VMEM(cube, jnp.int32), pltpu.VMEM(flat, jnp.int32), pltpu.SMEM((16,), F32),
                 pltpu.VMEM((16, 80, 128), F32), pltpu.SemaphoreType.DMA((12,))),
        specs=[HB] * 6, name="inside", flops=10**7, moved=2 * 10**6,
    )(*(pltpu.with_memory_space_constraint(x, pltpu.HBM) for x in (t, liquid, depth, now, prior, mix)))
    planes = [pltpu.VMEM((20 * 16, 128), BF16)] * 3
    ra = swap(pa, LAT_A)
    v1, v2, v3, gp = call(
        ahead, (shape(128, 144, dtype=BF16), shape(512, 128, dtype=BF16), shape(16, 512, dtype=BF16), shape(256, 128)),
        scratch=planes, specs=[VM] * 4, name="ahead", flops=10**6, moved=10**5,
    )(fk, w1, w2, w3)
    pb, gp = lax.optimization_barrier((pb, gp))
    rb = swap(pb, LAT_B)
    g1, rt, rf = call(middle_rows, (shape(*inner), shape(*flat), shape(*flat)), scratch=planes,
                      specs=[VM] * 7, name="middle_rows", flops=10**9, moved=10**6,
                      )(fk, tv, wet, v1, v2, v3, gp)
    e4, fb, dd, rfx, qa, qb = call(
        between,
        (shape(4, 80, 128), shape(64, 128), shape(32, 128), shape(*tall), shape(*tall), shape(96, 128)),
        specs=[VM] * 9, name="between", flops=10**7, moved=10**6,
    )(ra, rb, own, fk, fc, rt, rf, both, mx)
    hb = swap(qb, LON_B)
    ha = swap(qa, LON_A)
    g2 = call(outer_rows, shape(512, 128), scratch=planes, specs=[VM] * 6, name="outer_rows",
              flops=5 * 10**8, moved=10**6)(fk, fb, v1, v2, v3, g1)
    return call(
        closing,
        (shape(*cube), shape(*flat), shape(*flat)),
        scratch=(pltpu.VMEM(cube, F32), pltpu.VMEM((2, 64, 128), F32), pltpu.SemaphoreType.DMA((6,))),
        specs=[VM] * 15, out_specs=(HB, HB, HB), name="closing", flops=10**8, moved=3 * 10**6,
    )(qa, qb, ha, hb, rfx, e4, dd, warm, wet, g1, g2, w1, v2, v3, mx)


def solution(mesh):
    wide, flat = P(None, "lat", "lon"), P("lat", "lon")
    return jax.shard_map(
        on_device,
        mesh=mesh,
        in_specs=(wide, flat, flat, wide, flat, P(), P(), P(), P()),
        out_specs=(wide, flat, flat),
        check_vma=False,
    )
```

```python
import functools

import jax
import jax.numpy as jnp
from jax import lax
from jax.experimental import pallas as pl
from jax.experimental.pallas import tpu as pltpu
from jax.sharding import PartitionSpec as P

SUB = 8
F32 = jnp.float32
BF16 = jnp.bfloat16
C0 = 0.7978845608028654
C1 = 0.044715 * C0
DRY = 1e30
VM = pl.BlockSpec(memory_space=pltpu.VMEM)
HB = pl.BlockSpec(memory_space=pltpu.HBM)
NT = (((1,), (1,)), ((), ()))


def iota(shape, axis):
    return lax.broadcasted_iota(jnp.int32, shape, axis)


def roll(x, shift, axis):
    size = x.shape[axis]
    shift = shift % size
    return x if shift == 0 else pltpu.roll(x, shift, axis)


def lanes_from(x, index):
    return jnp.take_along_axis(x, index, axis=1)


def gelu_twice(x):
    return x + x * jnp.tanh(x * (C0 + C1 * (x * x)))


def call(body, outs, scratch=(), specs=None, out_specs=None, flops=0, moved=0, room=40, **given):
    return pl.pallas_call(
        body,
        out_shape=outs,
        in_specs=specs,
        out_specs=out_specs or jax.tree.map(lambda _: VM, outs),
        scratch_shapes=list(scratch),
        compiler_params=pltpu.CompilerParams(vmem_limit_bytes=room * 1024 * 1024),
        cost_estimate=pl.CostEstimate(flops=flops, bytes_accessed=moved, transcendentals=0),
        **given,
    )


def shape(*dims, dtype=F32):
    return jax.ShapeDtypeStruct(dims, dtype)


def inside(t_hbm, l_hbm, d_hbm, now_hbm, prior_hbm, mix_hbm,
           t_ref, warm_ref, wet_ref, fk_ref, fc_ref, own_ref, np_ref, mx_ref, pa_ref, pb_ref,
           l_ref, d_ref, mix_ref, q_ref, sems):
    lat = lax.axis_index("lat")
    copies = [pltpu.make_async_copy(d_hbm, d_ref, sems.at[0]), pltpu.make_async_copy(mix_hbm, mix_ref, sems.at[1])]
    for c in range(4):
        part = pl.ds(4 * c, 4)
        copies.append(pltpu.make_async_copy(t_hbm.at[part], t_ref.at[part], sems.at[2 + 2 * c]))
        copies.append(pltpu.make_async_copy(l_hbm.at[part], l_ref.at[part], sems.at[3 + 2 * c]))
    copies.append(pltpu.make_async_copy(now_hbm, np_ref.at[0], sems.at[10]))
    copies.append(pltpu.make_async_copy(prior_hbm, np_ref.at[1], sems.at[11]))
    for copy in copies:
        copy.start()
    dims = (64, 128)
    lane = iota(dims, 1)
    q_ref[:, 0:8, :] = jnp.full((16, 8, 128), DRY, F32)
    q_ref[:, 72:80, :] = jnp.full((16, 8, 128), DRY, F32)
    column = jnp.zeros(dims, F32)
    forcing = jnp.zeros(dims, F32)
    copies[0].wait()
    copies[1].wait()
    depth = d_ref[...]
    for k in range(16):
        if k % 4 == 0:
            copies[2 + k // 2].wait()
            copies[3 + k // 2].wait()
        t = t_ref[k]
        water = (l_ref[k] > 0) & (k < depth)
        q = jnp.where(water, t, DRY)
        q_ref[k, 8:72, :] = q
        wet = jnp.where(water, 1.0, 0.0).astype(F32)
        wet_ref[k] = wet

        def term(n):
            return jnp.where(n < DRY, n - t, 0.0)

        east = jnp.where(lane == 127, DRY, roll(q, 127, 1))
        west = jnp.where(lane == 0, DRY, roll(q, 1, 1))
        inflow = (term(q_ref[k, 7:71, :]) + term(q_ref[k, 9:73, :])) + (term(west) + term(east))
        warm = t + mix_ref[k] * jnp.where(water, inflow, 0.0)
        feature = jnp.where(water, warm, 0.0)
        warm_ref[k] = warm
        fk_ref[pl.ds(k, 64, stride=16), :] = feature
        column = column + wet
        forcing = forcing + feature
    forcing = 0.01 * forcing
    fc_ref[0] = forcing
    fc_ref[1] = column

    copies[10].wait()
    copies[11].wait()
    level, lane16 = iota((24, 128), 0), iota((24, 128), 1)
    mx = jnp.zeros((24, 128), F32)
    for k in range(16):
        mx = jnp.where((level == k) | ((level == 16) & (lane16 == k)), mix_ref[k], mx)
    mx_ref[...] = mx

    def payload(r, first):
        own = jnp.concatenate([t_ref[:, r, :], wet_ref[:, r, :]], axis=0)
        feature = fk_ref[16 * r : 16 * r + 16, :]
        rows = [x[first : first + 8] for x in (forcing, column, np_ref[0], np_ref[1])]
        return own, jnp.concatenate([own, feature] + rows + [edge_pairs(t_ref, wet_ref, first)], axis=0)

    own_low, low = payload(0, 0)
    own_high, high = payload(63, 56)
    own_ref[...] = jnp.concatenate([own_low, own_high], axis=0)
    even = lat % 2 == 0
    pa_ref[...] = jnp.where(even, high, low)
    pb_ref[...] = jnp.where(even, low, high)

    @pl.when(lat == 7)
    def _():
        small = (8, 128)
        back = 127 - iota(small, 1)
        swap = iota(small, 1) ^ 1
        for i in range(11):
            x = high[8 * i : 8 * i + 8]
            x = lanes_from(x, swap if i == 10 else back)
            if i >= 6:
                x = jnp.concatenate([x[j : j + 1] for j in range(7, -1, -1)], axis=0)
            pb_ref[8 * i : 8 * i + 8, :] = x


def edge_pairs(t_ref, wet_ref, first):
    pair = iota((8, 128), 1) >> 1
    rt = jnp.zeros((8, 128), F32)
    for k in range(16):
        rt = jnp.where(pair == k, roll(t_ref[k, first : first + 8, :], 2 * k + 1, 1), rt)
        rt = jnp.where(pair == 16 + k, roll(wet_ref[k, first : first + 8, :], 33 + 2 * k, 1), rt)
    return rt


def edge_features(fk_ref, first):
    part = iota((8, 128), 1) >> 3
    rf = jnp.zeros((8, 128), F32)
    for k in range(16):
        rf = jnp.where(part == k, roll(fk_ref[pl.ds(16 * first + k, 8, stride=16), :], 8 * k + 4, 1), rf)
    return rf


def between(pa_ref, pb_ref, own_ref, fk_ref, fc_ref, rt_ref, rf_ref, np_ref, mx_ref,
            e4_ref, fb_ref, dd_ref, rfx_ref, qa_ref, qb_ref):
    lat = lax.axis_index("lat")
    even = lat % 2 == 0
    pa, pb = pa_ref[...], pb_ref[...]
    high = jnp.where(even, pa, pb)
    low = jnp.where(lat == 0, 0.0, jnp.where(even, pb, pa))
    level, lane16 = iota((16, 128), 0), iota((16, 128), 1)
    mix = mx_ref[0:16, :]

    def delta(halo, first):
        t, wet = own_ref[first : first + 16, :], own_ref[first + 16 : first + 32, :]
        return mix * (wet * halo[16:32]) * (halo[0:16] - t)

    d_low, d_high = delta(low, 0), delta(high, 32)
    dd_ref[0:16, :] = d_low
    dd_ref[16:32, :] = d_high
    f_out_low, f_low = low[32:48] - d_low, fk_ref[0:16, :] + d_low
    f_high, f_out_high = fk_ref[1008:1024, :] + d_high, high[32:48] - d_high
    fb_ref[...] = jnp.concatenate([f_out_low, f_low, f_high, f_out_high], axis=0)
    s_low = 0.01 * jnp.sum(d_low, axis=0, keepdims=True)
    s_high = 0.01 * jnp.sum(d_high, axis=0, keepdims=True)

    ext = (80, 128)
    lane, row = iota(ext, 1), iota(ext, 0)

    def extend(i, middle):
        first = 48 + 8 * i
        return jnp.concatenate([low[first : first + 8], middle, high[first : first + 8]], axis=0)

    forcing = extend(0, fc_ref[0])
    forcing = forcing + jnp.where(row == 8, s_low, 0.0) - jnp.where(row == 7, s_low, 0.0)
    forcing = forcing + jnp.where(row == 71, s_high, 0.0) - jnp.where(row == 72, s_high, 0.0)
    fields = [forcing, extend(1, fc_ref[1]), extend(2, np_ref[0]), extend(3, np_ref[1])]
    mixed = extend(4, rt_ref[...])
    for i, field in enumerate(fields):
        e4_ref[i] = field
        mixed = jnp.where(lane >> 4 == 4 + i, roll(field, 72 + 16 * i, 1), mixed)

    def laid(f):
        x = pltpu.roll(f, 4, 1, stride=8, stride_axis=0)
        return jnp.sum(jnp.where(lane16 >> 3 == level, x, 0.0), axis=0, keepdims=True)

    zero = jnp.zeros((8, 128), F32)
    rf = jnp.concatenate([zero, rf_ref[...], zero], axis=0)
    for at, f in ((7, f_out_low), (8, f_low), (71, f_high), (72, f_out_high)):
        rf = jnp.where(row == at, laid(f), rf)
    rfx_ref[...] = rf

    small = iota((8, 128), 1)

    def columns(side):
        wide = 64 + 16 * ((small - 64) >> 3) + 8 * side + (small & 7)
        index = jnp.where(small < 32, 2 * small + side, jnp.where(small < 64, 0, wide))
        index_f = jnp.where((small >= 32) & (small < 48), 8 * (small - 32) + 3 + side, 0)
        parts = []
        for i in range(10):
            a = lanes_from(mixed[8 * i : 8 * i + 8], index)
            b = lanes_from(rf[8 * i : 8 * i + 8], index_f)
            parts.append(jnp.where((small >= 32) & (small < 48), b, a))
        return jnp.concatenate(parts, axis=0)

    first_core = lax.axis_index("lon") % 2 == 0
    q_east, q_west = columns(0), columns(1)
    qa_ref[...] = jnp.where(first_core, q_east, q_west)
    qb_ref[0:80, :] = jnp.where(first_core, q_west, q_east)
    qb_ref[80:96, :] = jnp.zeros((16, 128), F32)


def layers(w1, w2, w3, window):
    h = gelu_twice(jnp.dot(w1, window, preferred_element_type=F32)).astype(BF16)
    y = gelu_twice(jnp.dot(w2, h, preferred_element_type=F32)).astype(BF16)
    net = jnp.dot(w3, y, preferred_element_type=F32)
    return 0.5 * net.astype(BF16).astype(F32)


def put(planes, at, x):
    n = x.shape[0]
    for plane, shift in zip(planes, (1, 0, 127)):
        plane[at : at + n, :] = roll(x, shift, 1).astype(BF16)


def chunk(weights, planes, starts, g_ref, at):
    w1, w2, w3 = (w[...] for w in weights)
    windows = [jnp.concatenate([f[16 * r : 16 * r + 48, :] for f in planes], axis=0) for r in starts]
    net = layers(w1, w2, w3, jnp.concatenate(windows, axis=1))
    for i in range(16):
        g_ref[16 * (at + i) : 16 * (at + i) + 16, :] = net[:, 128 * i : 128 * i + 128]


def inner_chunk(fk_ref, weights, planes, c, g_ref, at):
    put(planes, 0, fk_ref[16 * (7 + 16 * c) : 16 * (25 + 16 * c), :])
    chunk(weights, planes, list(range(16)), g_ref, at)


def early_rows():
    lon, lat = lax.axis_index("lon"), lax.axis_index("lat")
    place = (lon % 16) // 2
    return (lat == 7) & (place <= 2)


def late_rows():
    return lax.axis_index("lon") % 16 >= 14


def ahead(fk_ref, w1_ref, w2_ref, w3_ref, w1_out, w2_out, w3_out, g_ref, *planes):
    w1 = jnp.concatenate([w1_ref[3 * a + b] for b in range(3) for a in range(3)], axis=0)
    w1_out[...] = w1.astype(F32).T.astype(BF16)
    w2_out[...] = (w2_ref[...].astype(F32) * 0.5).astype(BF16)
    w3_out[...] = (w3_ref[...].astype(F32) * 0.5).astype(BF16)
    weights = (w1_out, w2_out, w3_out)
    pl.when(early_rows())(functools.partial(inner_chunk, fk_ref, weights, planes, 0, g_ref, 0))


def middle_rows(fk_ref, t_ref, wet_ref, w1_ref, w2_ref, w3_ref, done_ref, g_ref, rt_ref, rf_ref, *planes):
    weights = (w1_ref, w2_ref, w3_ref)
    early = early_rows()
    pl.when(jnp.logical_not(early))(functools.partial(inner_chunk, fk_ref, weights, planes, 0, g_ref, 0))

    @pl.when(early)
    def _():
        g_ref[0:256, :] = done_ref[...]

    pl.when(jnp.logical_not(late_rows()))(functools.partial(inner_chunk, fk_ref, weights, planes, 1, g_ref, 16))
    for i in range(0, 64, 8):
        rt_ref[i : i + 8, :] = edge_pairs(t_ref, wet_ref, i)
        rf_ref[i : i + 8, :] = edge_features(fk_ref, i)
    inner_chunk(fk_ref, weights, planes, 2, g_ref, 32)


def outer_rows(fk_ref, fb_ref, w1_ref, w2_ref, w3_ref, g1_ref, g_ref, *planes):
    weights = (w1_ref, w2_ref, w3_ref)
    late = late_rows()
    pl.when(late)(functools.partial(inner_chunk, fk_ref, weights, planes, 1, g_ref, 16))

    @pl.when(jnp.logical_not(late))
    def _():
        g_ref[256:512, :] = g1_ref[256:512, :]

    put(planes, 0, fb_ref[0:32, :])
    put(planes, 16 * 2, fk_ref[16 : 16 * 9, :])
    put(planes, 16 * 10, fk_ref[16 * 55 : 16 * 63, :])
    put(planes, 16 * 18, fb_ref[32:64, :])
    chunk(weights, planes, [r + 2 * (r >= 8) for r in range(16)], g_ref, 0)


def closing(qa_ref, qb_ref, ha_ref, hb_ref, rf_ref, e4_ref, dd_ref, warm_ref, wet_ref,
            g1_ref, g2_ref, w1_ref, w2_ref, w3_ref, mx_ref, out_hbm, eta_hbm, mid_hbm, out_ref, eta_ref, sems):
    first_core = lax.axis_index("lon") % 2 == 0
    ext = (80, 128)
    lane = iota(ext, 1)
    small, sub = iota((8, 128), 1), iota((8, 128), 0)
    qa, qb, ha, hb = qa_ref[...], qb_ref[0:80, :], ha_ref[...], hb_ref[0:80, :]
    q_west, q_east = jnp.where(first_core, qb, qa), jnp.where(first_core, qa, qb)
    h_west, h_east = jnp.where(first_core, hb, ha), jnp.where(first_core, ha, hb)
    mix = mx_ref[16:17, :]

    def delta(halo, own):
        return mix * roll(halo * own, 112, 1) * (halo - own)

    d_west, d_east = delta(h_west, q_west), delta(h_east, q_east)

    rf = rf_ref[...]
    index_w = jnp.where(small < 64, 8 * (small & 15) + 3 + (small >> 4), 0)
    index_e = jnp.where(small < 64, 8 * (small & 15) + 1 + (small >> 4), 0)
    f_west = jnp.concatenate([lanes_from(rf[8 * i : 8 * i + 8], index_w) for i in range(10)], axis=0)
    f_east = jnp.concatenate([lanes_from(rf[8 * i : 8 * i + 8], index_e) for i in range(10)], axis=0)
    which = lane >> 4
    f_west = jnp.where(which == 0, roll(h_west, 96, 1) - d_west,
                       f_west + jnp.where(which == 1, roll(d_west, 16, 1), 0.0))
    f_east = jnp.where(which == 3, roll(h_east, 16, 1) - roll(d_east, 48, 1),
                       f_east + jnp.where(which == 2, roll(d_east, 32, 1), 0.0))
    cells = [f_east, roll(f_east, 112, 1), f_west, roll(f_west, 112, 1)]
    blank = jnp.zeros((80, 128), BF16)
    x = jnp.zeros((256, 128), F32)
    for a in range(3):
        window = jnp.concatenate([c[7 + a : 71 + a] for c in cells], axis=0).astype(BF16)
        w = jnp.concatenate([w1_ref[3 * a + b] for b in range(3)] + [blank], axis=0)
        x = x + jnp.dot(window, w, preferred_element_type=F32)

    side = []
    for i in range(4):
        east = roll(h_east, 128 - (64 + 8 * i), 1)
        west = roll(h_west, 56 - 8 * i, 1)
        side.append(jnp.where(lane < 8, east, jnp.where(lane >= 120, west, 0.0)))
    main = [e4_ref[i] for i in range(4)]
    s_west = 0.01 * jnp.sum(d_west, axis=1, keepdims=True)
    s_east = 0.01 * jnp.sum(d_east, axis=1, keepdims=True)
    push = [main[0] + jnp.where(lane == 0, s_west, 0.0) + jnp.where(lane == 127, s_east, 0.0),
            side[0] - jnp.where(lane == 127, s_west, 0.0) - jnp.where(lane == 0, s_east, 0.0)]
    speed = [0.45 * x / 16 for x in (main[1], side[1])]

    def neighbours(pair):
        out = []
        for i in range(2):
            x, other = pair[i], pair[1 - i]
            out.append((roll(jnp.where(lane == 0, other, x), 127, 1),
                        roll(jnp.where(lane == 127, other, x), 1, 1),
                        roll(x, 79, 0), roll(x, 1, 0)))
        return out

    active = [jnp.where(s > 0.0, 1.0, 0.0).astype(F32) for s in speed]
    facing = [[jnp.minimum(s, n) for n in ns] for s, ns in zip(speed, neighbours(speed))]

    def advance(current, earlier):
        fresh = []
        for i, ns in enumerate(neighbours(current)):
            c = current[i]
            change = 2.0 * c - earlier[i] + push[i]
            for f, n in zip(facing[i], ns):
                change = change + f * (n - c)
            fresh.append(active[i] * change)
        return fresh, current

    state = ([main[2], side[2]], [main[3], side[3]])

    h = gelu_twice(x).astype(BF16)
    x = lax.dot_general(h, w2_ref[...], NT, preferred_element_type=F32)
    state = advance(*state)
    state = advance(*state)
    y = gelu_twice(x).astype(BF16)
    w3 = jnp.concatenate([w3_ref[...], jnp.zeros((112, 512), BF16)], axis=0)
    net = lax.dot_general(y, w3, NT, preferred_element_type=F32)
    for _ in range(SUB - 2):
        state = advance(*state)
    eta_ref[0] = state[0][0][8:72]
    eta_ref[1] = state[1][0][8:72]
    copies = [pltpu.make_async_copy(eta_ref.at[0], eta_hbm, sems.at[4]),
              pltpu.make_async_copy(eta_ref.at[1], mid_hbm, sems.at[5])]
    copies[0].start()
    copies[1].start()

    net = 0.5 * net.astype(BF16).astype(F32)
    ends = [net[64 * c : 64 * c + 64] for c in range(4)]
    low16 = lane[:64] < 16
    ends[1] = ends[1] + jnp.where(low16, d_east[8:72], 0.0)
    ends[2] = ends[2] + jnp.where(low16, d_west[8:72], 0.0)
    spread = jnp.where(small < 64, small >> 2, 0)
    edges = []
    for i in range(8):
        x = jnp.zeros((8, 128), F32)
        for c in range(4):
            x = jnp.where(small & 3 == c, lanes_from(ends[c][8 * i : 8 * i + 8], spread), x)
        edges.append(x)

    at_edge = (small < 2) | (small >= 126)
    for k in range(16):
        for i in range(8):
            if i == 0 or i == 7:
                g = g2_ref[pl.ds((0 if i == 0 else 128) + k, 8, stride=16), :]
            elif i == 3 or i == 4:
                g = g2_ref[pl.ds((8 * i - 8) * 16 + k, 8, stride=16), :]
            else:
                g = g1_ref[pl.ds((8 * i - 8) * 16 + k, 8, stride=16), :]
            g = jnp.where(at_edge, roll(edges[i], 126 - 4 * k, 1), g)
            y = warm_ref[k, 8 * i : 8 * i + 8, :] + wet_ref[k, 8 * i : 8 * i + 8, :] * g
            if i == 0:
                y = y + jnp.where(sub == 0, dd_ref[k : k + 1, :], 0.0)
            if i == 7:
                y = y + jnp.where(sub == 7, dd_ref[16 + k : 17 + k, :], 0.0)
            out_ref[k, 8 * i : 8 * i + 8, :] = y
        if k % 4 == 3:
            part = pl.ds(k - 3, 4)
            copies.append(pltpu.make_async_copy(out_ref.at[part], out_hbm.at[part], sems.at[k // 4]))
            copies[-1].start()
    for copy in copies:
        copy.wait()


def partners(partner):
    pairs = []
    for lon in range(32):
        for lat in range(8):
            to = partner(lon, lat)
            pairs.append((8 * lon + lat, 8 * (to[0] % 32) + to[1]))
    return pairs


LAT_A = partners(lambda lon, lat: (lon, lat ^ 1))
LAT_B = partners(
    lambda lon, lat: (31 - lon, 7) if lat == 7 else (lon ^ 1, 0) if lat == 0 else (lon, lat + 1 if lat % 2 else lat - 1)
)
LON_A = partners(lambda lon, lat: (lon ^ 1, lat))
LON_B = partners(lambda lon, lat: (lon + 1 if lon % 2 else lon - 1, lat))


def swap(x, pairs):
    return lax.ppermute(x, ("lon", "lat"), pairs)


def on_device(t, now, prior, liquid, depth, mix, w1, w2, w3):
    w1 = jnp.transpose(w1, (0, 2, 1))
    cube, flat, tall, inner = (16, 64, 128), (64, 128), (80, 128), (768, 128)
    tv, warm, wet, fk, fc, own, both, mx, pa, pb = call(
        inside,
        (shape(*cube), shape(*cube), shape(*cube), shape(1024, 128), shape(2, 64, 128),
         shape(*flat), shape(2, 64, 128), shape(24, 128), shape(88, 128), shape(88, 128)),
        scratch=(pltpu.VMEM(cube, jnp.int32), pltpu.VMEM(flat, jnp.int32), pltpu.SMEM((16,), F32),
                 pltpu.VMEM((16, 80, 128), F32), pltpu.SemaphoreType.DMA((12,))),
        specs=[HB] * 6, name="inside", flops=10**7, moved=2 * 10**6,
    )(*(pltpu.with_memory_space_constraint(x, pltpu.HBM) for x in (t, liquid, depth, now, prior, mix)))
    planes = [pltpu.VMEM((20 * 16, 128), BF16)] * 3
    ra = swap(pa, LAT_A)
    v1, v2, v3, gp = call(
        ahead, (shape(128, 144, dtype=BF16), shape(512, 128, dtype=BF16), shape(16, 512, dtype=BF16), shape(256, 128)),
        scratch=planes, specs=[VM] * 4, name="ahead", flops=10**6, moved=10**5,
    )(fk, w1, w2, w3)
    pb, gp = lax.optimization_barrier((pb, gp))
    rb = swap(pb, LAT_B)
    g1, rt, rf = call(middle_rows, (shape(*inner), shape(*flat), shape(*flat)), scratch=planes,
                      specs=[VM] * 7, name="middle_rows", flops=10**9, moved=10**6,
                      )(fk, tv, wet, v1, v2, v3, gp)
    e4, fb, dd, rfx, qa, qb = call(
        between,
        (shape(4, 80, 128), shape(64, 128), shape(32, 128), shape(*tall), shape(*tall), shape(96, 128)),
        specs=[VM] * 9, name="between", flops=10**7, moved=10**6,
    )(ra, rb, own, fk, fc, rt, rf, both, mx)
    hb = swap(qb, LON_B)
    ha = swap(qa, LON_A)
    g2 = call(outer_rows, shape(512, 128), scratch=planes, specs=[VM] * 6, name="outer_rows",
              flops=5 * 10**8, moved=10**6)(fk, fb, v1, v2, v3, g1)
    return call(
        closing,
        (shape(*cube), shape(*flat), shape(*flat)),
        scratch=(pltpu.VMEM(cube, F32), pltpu.VMEM((2, 64, 128), F32), pltpu.SemaphoreType.DMA((6,))),
        specs=[VM] * 15, out_specs=(HB, HB, HB), name="closing", flops=10**8, moved=3 * 10**6,
    )(qa, qb, ha, hb, rfx, e4, dd, warm, wet, g1, g2, w1, v2, v3, mx)


def solution(mesh):
    wide, flat = P(None, "lat", "lon"), P("lat", "lon")
    return jax.shard_map(
        on_device,
        mesh=mesh,
        in_specs=(wide, flat, flat, wide, flat, P(), P(), P(), P()),
        out_specs=(wide, flat, flat),
        check_vma=False,
    )
```

```python
import functools

import jax
import jax.numpy as jnp
from jax import lax
from jax.experimental import pallas as pl
from jax.experimental.pallas import tpu as pltpu
from jax.sharding import PartitionSpec as P

SUB = 8
F32 = jnp.float32
BF16 = jnp.bfloat16
C0 = 0.7978845608028654
C1 = 0.044715 * C0
DRY = 1e30
VM = pl.BlockSpec(memory_space=pltpu.VMEM)
HB = pl.BlockSpec(memory_space=pltpu.HBM)
NT = (((1,), (1,)), ((), ()))


def iota(shape, axis):
    return lax.broadcasted_iota(jnp.int32, shape, axis)


def roll(x, shift, axis):
    size = x.shape[axis]
    shift = shift % size
    return x if shift == 0 else pltpu.roll(x, shift, axis)


def lanes_from(x, index):
    return jnp.take_along_axis(x, index, axis=1)


def gelu_twice(x):
    return x + x * jnp.tanh(x * (C0 + C1 * (x * x)))


def call(body, outs, scratch=(), specs=None, out_specs=None, flops=0, moved=0, room=40, **given):
    return pl.pallas_call(
        body,
        out_shape=outs,
        in_specs=specs,
        out_specs=out_specs or jax.tree.map(lambda _: VM, outs),
        scratch_shapes=list(scratch),
        compiler_params=pltpu.CompilerParams(vmem_limit_bytes=room * 1024 * 1024),
        cost_estimate=pl.CostEstimate(flops=flops, bytes_accessed=moved, transcendentals=0),
        **given,
    )


def shape(*dims, dtype=F32):
    return jax.ShapeDtypeStruct(dims, dtype)


def inside(t_hbm, l_hbm, d_hbm, now_hbm, prior_hbm, mix_hbm,
           t_ref, warm_ref, wet_ref, fk_ref, fc_ref, own_ref, np_ref, mx_ref, pa_ref, pb_ref,
           l_ref, d_ref, mix_ref, q_ref, sems):
    lat = lax.axis_index("lat")
    copies = [pltpu.make_async_copy(d_hbm, d_ref, sems.at[0]), pltpu.make_async_copy(mix_hbm, mix_ref, sems.at[1])]
    for c in range(4):
        part = pl.ds(4 * c, 4)
        copies.append(pltpu.make_async_copy(t_hbm.at[part], t_ref.at[part], sems.at[2 + 2 * c]))
        copies.append(pltpu.make_async_copy(l_hbm.at[part], l_ref.at[part], sems.at[3 + 2 * c]))
    copies.append(pltpu.make_async_copy(now_hbm, np_ref.at[0], sems.at[10]))
    copies.append(pltpu.make_async_copy(prior_hbm, np_ref.at[1], sems.at[11]))
    for copy in copies:
        copy.start()
    dims = (64, 128)
    lane = iota(dims, 1)
    q_ref[:, 0:8, :] = jnp.full((16, 8, 128), DRY, F32)
    q_ref[:, 72:80, :] = jnp.full((16, 8, 128), DRY, F32)
    column = jnp.zeros(dims, F32)
    forcing = jnp.zeros(dims, F32)
    copies[0].wait()
    copies[1].wait()
    depth = d_ref[...]
    for k in range(16):
        if k % 4 == 0:
            copies[2 + k // 2].wait()
            copies[3 + k // 2].wait()
        t = t_ref[k]
        water = (l_ref[k] > 0) & (k < depth)
        q = jnp.where(water, t, DRY)
        q_ref[k, 8:72, :] = q
        wet = jnp.where(water, 1.0, 0.0).astype(F32)
        wet_ref[k] = wet

        def term(n):
            return jnp.where(n < DRY, n - t, 0.0)

        east = jnp.where(lane == 127, DRY, roll(q, 127, 1))
        west = jnp.where(lane == 0, DRY, roll(q, 1, 1))
        inflow = (term(q_ref[k, 7:71, :]) + term(q_ref[k, 9:73, :])) + (term(west) + term(east))
        warm = t + mix_ref[k] * jnp.where(water, inflow, 0.0)
        feature = jnp.where(water, warm, 0.0)
        warm_ref[k] = warm
        fk_ref[pl.ds(k, 64, stride=16), :] = feature
        column = column + wet
        forcing = forcing + feature
    forcing = 0.01 * forcing
    fc_ref[0] = forcing
    fc_ref[1] = column

    copies[10].wait()
    copies[11].wait()
    level, lane16 = iota((24, 128), 0), iota((24, 128), 1)
    mx = jnp.zeros((24, 128), F32)
    for k in range(16):
        mx = jnp.where((level == k) | ((level == 16) & (lane16 == k)), mix_ref[k], mx)
    mx_ref[...] = mx

    def payload(r, first):
        own = jnp.concatenate([t_ref[:, r, :], wet_ref[:, r, :]], axis=0)
        feature = fk_ref[16 * r : 16 * r + 16, :]
        rows = [x[first : first + 8] for x in (forcing, column, np_ref[0], np_ref[1])]
        pairs = edge_pairs(t_ref, wet_ref, first)
        return jnp.concatenate([own, pairs], axis=0), jnp.concatenate([own, feature] + rows + [pairs], axis=0)

    own_low, low = payload(0, 0)
    own_high, high = payload(63, 56)
    own_ref[...] = jnp.concatenate([own_low[0:32], own_high[0:32], own_low[32:40], own_high[32:40]], axis=0)
    even = lat % 2 == 0
    pa_ref[...] = jnp.where(even, high, low)
    pb_ref[...] = jnp.where(even, low, high)

    @pl.when(lat == 7)
    def _():
        small = (8, 128)
        back = 127 - iota(small, 1)
        swap = iota(small, 1) ^ 1
        for i in range(11):
            x = high[8 * i : 8 * i + 8]
            x = lanes_from(x, swap if i == 10 else back)
            if i >= 6:
                x = jnp.concatenate([x[j : j + 1] for j in range(7, -1, -1)], axis=0)
            pb_ref[8 * i : 8 * i + 8, :] = x


def edge_pairs(t_ref, wet_ref, first):
    pair = iota((8, 128), 1) >> 1
    rt = jnp.zeros((8, 128), F32)
    for k in range(16):
        rt = jnp.where(pair == k, roll(t_ref[k, first : first + 8, :], 2 * k + 1, 1), rt)
        rt = jnp.where(pair == 16 + k, roll(wet_ref[k, first : first + 8, :], 33 + 2 * k, 1), rt)
    return rt


def edge_features(fk_ref, first):
    part = iota((8, 128), 1) >> 3
    rf = jnp.zeros((8, 128), F32)
    for k in range(16):
        rf = jnp.where(part == k, roll(fk_ref[pl.ds(16 * first + k, 8, stride=16), :], 8 * k + 4, 1), rf)
    return rf


def between(pa_ref, pb_ref, own_ref, fk_ref, fc_ref, rt_ref, rf_ref, np_ref, mx_ref,
            e4_ref, fb_ref, dd_ref, rfx_ref, qa_ref, qb_ref):
    lat = lax.axis_index("lat")
    even = lat % 2 == 0
    pa, pb = pa_ref[...], pb_ref[...]
    high = jnp.where(even, pa, pb)
    low = jnp.where(lat == 0, 0.0, jnp.where(even, pb, pa))
    level, lane16 = iota((16, 128), 0), iota((16, 128), 1)
    mix = mx_ref[0:16, :]

    def delta(halo, first):
        t, wet = own_ref[first : first + 16, :], own_ref[first + 16 : first + 32, :]
        return mix * (wet * halo[16:32]) * (halo[0:16] - t)

    d_low, d_high = delta(low, 0), delta(high, 32)
    dd_ref[0:16, :] = d_low
    dd_ref[16:32, :] = d_high
    f_out_low, f_low = low[32:48] - d_low, fk_ref[0:16, :] + d_low
    f_high, f_out_high = fk_ref[1008:1024, :] + d_high, high[32:48] - d_high
    fb_ref[...] = jnp.concatenate([f_out_low, f_low, f_high, f_out_high], axis=0)
    s_low = 0.01 * jnp.sum(d_low, axis=0, keepdims=True)
    s_high = 0.01 * jnp.sum(d_high, axis=0, keepdims=True)

    ext = (80, 128)
    lane, row = iota(ext, 1), iota(ext, 0)

    def extend(i, middle):
        first = 48 + 8 * i
        return jnp.concatenate([low[first : first + 8], middle, high[first : first + 8]], axis=0)

    forcing = extend(0, fc_ref[0])
    forcing = forcing + jnp.where(row == 8, s_low, 0.0) - jnp.where(row == 7, s_low, 0.0)
    forcing = forcing + jnp.where(row == 71, s_high, 0.0) - jnp.where(row == 72, s_high, 0.0)
    fields = [forcing, extend(1, fc_ref[1]), extend(2, np_ref[0]), extend(3, np_ref[1])]
    mixed = extend(4, rt_ref[...])
    for i, field in enumerate(fields):
        e4_ref[i] = field
        mixed = jnp.where(lane >> 4 == 4 + i, roll(field, 72 + 16 * i, 1), mixed)

    def laid(f):
        x = pltpu.roll(f, 4, 1, stride=8, stride_axis=0)
        return jnp.sum(jnp.where(lane16 >> 3 == level, x, 0.0), axis=0, keepdims=True)

    zero = jnp.zeros((8, 128), F32)
    rf = jnp.concatenate([zero, rf_ref[...], zero], axis=0)
    for at, f in ((7, f_out_low), (8, f_low), (71, f_high), (72, f_out_high)):
        rf = jnp.where(row == at, laid(f), rf)
    rfx_ref[...] = rf

    small = iota((8, 128), 1)

    def columns(side):
        wide = 64 + 16 * ((small - 64) >> 3) + 8 * side + (small & 7)
        index = jnp.where(small < 32, 2 * small + side, jnp.where(small < 64, 0, wide))
        index_f = jnp.where((small >= 32) & (small < 48), 8 * (small - 32) + 3 + side, 0)
        parts = []
        for i in range(10):
            a = lanes_from(mixed[8 * i : 8 * i + 8], index)
            b = lanes_from(rf[8 * i : 8 * i + 8], index_f)
            parts.append(jnp.where((small >= 32) & (small < 48), b, a))
        return jnp.concatenate(parts, axis=0)

    first_core = lax.axis_index("lon") % 2 == 0
    q_east, q_west = columns(0), columns(1)
    qa_ref[...] = jnp.where(first_core, q_east, q_west)
    qb_ref[0:80, :] = jnp.where(first_core, q_west, q_east)
    qb_ref[80:96, :] = jnp.zeros((16, 128), F32)


def layers(w1, w2, w3, window):
    h = gelu_twice(jnp.dot(w1, window, preferred_element_type=F32)).astype(BF16)
    y = gelu_twice(jnp.dot(w2, h, preferred_element_type=F32)).astype(BF16)
    net = jnp.dot(w3, y, preferred_element_type=F32)
    return 0.5 * net.astype(BF16).astype(F32)


def put(planes, at, x):
    n = x.shape[0]
    for plane, shift in zip(planes, (1, 0, 127)):
        plane[at : at + n, :] = roll(x, shift, 1).astype(BF16)


def chunk(weights, planes, starts, g_ref, at):
    w1, w2, w3 = (w[...] for w in weights)
    windows = [jnp.concatenate([f[16 * r : 16 * r + 48, :] for f in planes], axis=0) for r in starts]
    net = layers(w1, w2, w3, jnp.concatenate(windows, axis=1))
    for i in range(16):
        g_ref[16 * (at + i) : 16 * (at + i) + 16, :] = net[:, 128 * i : 128 * i + 128]


def inner_chunk(fk_ref, weights, planes, c, g_ref, at):
    put(planes, 0, fk_ref[16 * (7 + 16 * c) : 16 * (25 + 16 * c), :])
    chunk(weights, planes, list(range(16)), g_ref, at)


def early_rows():
    lon, lat = lax.axis_index("lon"), lax.axis_index("lat")
    place = (lon % 16) // 2
    return (lat == 7) & (place <= 2)


def late_rows():
    return lax.axis_index("lon") % 16 >= 14


def ahead(fk_ref, w1_ref, w2_ref, w3_ref, w1_out, w2_out, w3_out, g_ref, *planes):
    w1 = jnp.concatenate([w1_ref[3 * a + b] for b in range(3) for a in range(3)], axis=0)
    w1_out[...] = w1.astype(F32).T.astype(BF16)
    w2_out[...] = (w2_ref[...].astype(F32) * 0.5).astype(BF16)
    w3_out[...] = (w3_ref[...].astype(F32) * 0.5).astype(BF16)
    weights = (w1_out, w2_out, w3_out)
    pl.when(early_rows())(functools.partial(inner_chunk, fk_ref, weights, planes, 0, g_ref, 0))


def middle_rows(fk_ref, t_ref, wet_ref, own_ref, w1_ref, w2_ref, w3_ref, done_ref, g_ref, rt_ref, rf_ref, *planes):
    weights = (w1_ref, w2_ref, w3_ref)
    early = early_rows()
    pl.when(jnp.logical_not(early))(functools.partial(inner_chunk, fk_ref, weights, planes, 0, g_ref, 0))

    @pl.when(early)
    def _():
        g_ref[0:256, :] = done_ref[...]

    pl.when(jnp.logical_not(late_rows()))(functools.partial(inner_chunk, fk_ref, weights, planes, 1, g_ref, 16))
    rt_ref[0:8, :] = own_ref[64:72, :]
    rt_ref[56:64, :] = own_ref[72:80, :]
    for i in range(0, 64, 8):
        if 0 < i < 56:
            rt_ref[i : i + 8, :] = edge_pairs(t_ref, wet_ref, i)
        rf_ref[i : i + 8, :] = edge_features(fk_ref, i)
    inner_chunk(fk_ref, weights, planes, 2, g_ref, 32)


def outer_rows(fk_ref, fb_ref, w1_ref, w2_ref, w3_ref, g1_ref, g_ref, *planes):
    weights = (w1_ref, w2_ref, w3_ref)
    late = late_rows()
    pl.when(late)(functools.partial(inner_chunk, fk_ref, weights, planes, 1, g_ref, 16))

    @pl.when(jnp.logical_not(late))
    def _():
        g_ref[256:512, :] = g1_ref[256:512, :]

    put(planes, 0, fb_ref[0:32, :])
    put(planes, 16 * 2, fk_ref[16 : 16 * 9, :])
    put(planes, 16 * 10, fk_ref[16 * 55 : 16 * 63, :])
    put(planes, 16 * 18, fb_ref[32:64, :])
    chunk(weights, planes, [r + 2 * (r >= 8) for r in range(16)], g_ref, 0)


def closing(qa_ref, qb_ref, ha_ref, hb_ref, rf_ref, e4_ref, dd_ref, warm_ref, wet_ref,
            g1_ref, g2_ref, w1_ref, w2_ref, w3_ref, mx_ref, out_hbm, eta_hbm, mid_hbm, out_ref, eta_ref, sems):
    first_core = lax.axis_index("lon") % 2 == 0
    ext = (80, 128)
    lane = iota(ext, 1)
    small, sub = iota((8, 128), 1), iota((8, 128), 0)
    qa, qb, ha, hb = qa_ref[...], qb_ref[0:80, :], ha_ref[...], hb_ref[0:80, :]
    q_west, q_east = jnp.where(first_core, qb, qa), jnp.where(first_core, qa, qb)
    h_west, h_east = jnp.where(first_core, hb, ha), jnp.where(first_core, ha, hb)
    mix = mx_ref[16:17, :]

    def delta(halo, own):
        return mix * roll(halo * own, 112, 1) * (halo - own)

    d_west, d_east = delta(h_west, q_west), delta(h_east, q_east)

    rf = rf_ref[...]
    index_w = jnp.where(small < 64, 8 * (small & 15) + 3 + (small >> 4), 0)
    index_e = jnp.where(small < 64, 8 * (small & 15) + 1 + (small >> 4), 0)
    f_west = jnp.concatenate([lanes_from(rf[8 * i : 8 * i + 8], index_w) for i in range(10)], axis=0)
    f_east = jnp.concatenate([lanes_from(rf[8 * i : 8 * i + 8], index_e) for i in range(10)], axis=0)
    which = lane >> 4
    f_west = jnp.where(which == 0, roll(h_west, 96, 1) - d_west,
                       f_west + jnp.where(which == 1, roll(d_west, 16, 1), 0.0))
    f_east = jnp.where(which == 3, roll(h_east, 16, 1) - roll(d_east, 48, 1),
                       f_east + jnp.where(which == 2, roll(d_east, 32, 1), 0.0))
    cells = [f_east, roll(f_east, 112, 1), f_west, roll(f_west, 112, 1)]
    blank = jnp.zeros((80, 128), BF16)
    x = jnp.zeros((256, 128), F32)
    for a in range(3):
        window = jnp.concatenate([c[7 + a : 71 + a] for c in cells], axis=0).astype(BF16)
        w = jnp.concatenate([w1_ref[3 * a + b] for b in range(3)] + [blank], axis=0)
        x = x + jnp.dot(window, w, preferred_element_type=F32)

    side = []
    for i in range(4):
        east = roll(h_east, 128 - (64 + 8 * i), 1)
        west = roll(h_west, 56 - 8 * i, 1)
        side.append(jnp.where(lane < 8, east, jnp.where(lane >= 120, west, 0.0)))
    main = [e4_ref[i] for i in range(4)]
    s_west = 0.01 * jnp.sum(d_west, axis=1, keepdims=True)
    s_east = 0.01 * jnp.sum(d_east, axis=1, keepdims=True)
    push = [main[0] + jnp.where(lane == 0, s_west, 0.0) + jnp.where(lane == 127, s_east, 0.0),
            side[0] - jnp.where(lane == 127, s_west, 0.0) - jnp.where(lane == 0, s_east, 0.0)]
    speed = [0.45 * x / 16 for x in (main[1], side[1])]

    def neighbours(pair):
        out = []
        for i in range(2):
            x, other = pair[i], pair[1 - i]
            out.append((roll(jnp.where(lane == 0, other, x), 127, 1),
                        roll(jnp.where(lane == 127, other, x), 1, 1),
                        roll(x, 79, 0), roll(x, 1, 0)))
        return out

    active = [jnp.where(s > 0.0, 1.0, 0.0).astype(F32) for s in speed]
    facing = [[jnp.minimum(s, n) for n in ns] for s, ns in zip(speed, neighbours(speed))]

    def advance(current, earlier):
        fresh = []
        for i, ns in enumerate(neighbours(current)):
            c = current[i]
            change = 2.0 * c - earlier[i] + push[i]
            for f, n in zip(facing[i], ns):
                change = change + f * (n - c)
            fresh.append(active[i] * change)
        return fresh, current

    state = ([main[2], side[2]], [main[3], side[3]])

    h = gelu_twice(x).astype(BF16)
    x = lax.dot_general(h, w2_ref[...], NT, preferred_element_type=F32)
    state = advance(*state)
    state = advance(*state)
    y = gelu_twice(x).astype(BF16)
    w3 = jnp.concatenate([w3_ref[...], jnp.zeros((112, 512), BF16)], axis=0)
    net = lax.dot_general(y, w3, NT, preferred_element_type=F32)
    for _ in range(SUB - 2):
        state = advance(*state)
    eta_ref[0] = state[0][0][8:72]
    eta_ref[1] = state[1][0][8:72]
    copies = [pltpu.make_async_copy(eta_ref.at[0], eta_hbm, sems.at[4]),
              pltpu.make_async_copy(eta_ref.at[1], mid_hbm, sems.at[5])]
    copies[0].start()
    copies[1].start()

    net = 0.5 * net.astype(BF16).astype(F32)
    ends = [net[64 * c : 64 * c + 64] for c in range(4)]
    low16 = lane[:64] < 16
    ends[1] = ends[1] + jnp.where(low16, d_east[8:72], 0.0)
    ends[2] = ends[2] + jnp.where(low16, d_west[8:72], 0.0)
    spread = jnp.where(small < 64, small >> 2, 0)
    edges = []
    for i in range(8):
        x = jnp.zeros((8, 128), F32)
        for c in range(4):
            x = jnp.where(small & 3 == c, lanes_from(ends[c][8 * i : 8 * i + 8], spread), x)
        edges.append(x)

    at_edge = (small < 2) | (small >= 126)
    for k in range(16):
        for i in range(8):
            if i == 0 or i == 7:
                g = g2_ref[pl.ds((0 if i == 0 else 128) + k, 8, stride=16), :]
            elif i == 3 or i == 4:
                g = g2_ref[pl.ds((8 * i - 8) * 16 + k, 8, stride=16), :]
            else:
                g = g1_ref[pl.ds((8 * i - 8) * 16 + k, 8, stride=16), :]
            g = jnp.where(at_edge, roll(edges[i], 126 - 4 * k, 1), g)
            y = warm_ref[k, 8 * i : 8 * i + 8, :] + wet_ref[k, 8 * i : 8 * i + 8, :] * g
            if i == 0:
                y = y + jnp.where(sub == 0, dd_ref[k : k + 1, :], 0.0)
            if i == 7:
                y = y + jnp.where(sub == 7, dd_ref[16 + k : 17 + k, :], 0.0)
            out_ref[k, 8 * i : 8 * i + 8, :] = y
        if k % 4 == 3:
            part = pl.ds(k - 3, 4)
            copies.append(pltpu.make_async_copy(out_ref.at[part], out_hbm.at[part], sems.at[k // 4]))
            copies[-1].start()
    for copy in copies:
        copy.wait()


def partners(partner):
    pairs = []
    for lon in range(32):
        for lat in range(8):
            to = partner(lon, lat)
            pairs.append((8 * lon + lat, 8 * (to[0] % 32) + to[1]))
    return pairs


LAT_A = partners(lambda lon, lat: (lon, lat ^ 1))
LAT_B = partners(
    lambda lon, lat: (31 - lon, 7) if lat == 7 else (lon ^ 1, 0) if lat == 0 else (lon, lat + 1 if lat % 2 else lat - 1)
)
LON_A = partners(lambda lon, lat: (lon ^ 1, lat))
LON_B = partners(lambda lon, lat: (lon + 1 if lon % 2 else lon - 1, lat))


def swap(x, pairs):
    return lax.ppermute(x, ("lon", "lat"), pairs)


def on_device(t, now, prior, liquid, depth, mix, w1, w2, w3):
    w1 = jnp.transpose(w1, (0, 2, 1))
    cube, flat, tall, inner = (16, 64, 128), (64, 128), (80, 128), (768, 128)
    tv, warm, wet, fk, fc, own, both, mx, pa, pb = call(
        inside,
        (shape(*cube), shape(*cube), shape(*cube), shape(1024, 128), shape(2, 64, 128),
         shape(*tall), shape(2, 64, 128), shape(24, 128), shape(88, 128), shape(88, 128)),
        scratch=(pltpu.VMEM(cube, jnp.int32), pltpu.VMEM(flat, jnp.int32), pltpu.SMEM((16,), F32),
                 pltpu.VMEM((16, 80, 128), F32), pltpu.SemaphoreType.DMA((12,))),
        specs=[HB] * 6, name="inside", flops=10**7, moved=2 * 10**6,
    )(*(pltpu.with_memory_space_constraint(x, pltpu.HBM) for x in (t, liquid, depth, now, prior, mix)))
    planes = [pltpu.VMEM((20 * 16, 128), BF16)] * 3
    ra = swap(pa, LAT_A)
    v1, v2, v3, gp = call(
        ahead, (shape(128, 144, dtype=BF16), shape(512, 128, dtype=BF16), shape(16, 512, dtype=BF16), shape(256, 128)),
        scratch=planes, specs=[VM] * 4, name="ahead", flops=10**6, moved=10**5,
    )(fk, w1, w2, w3)
    pb, gp = lax.optimization_barrier((pb, gp))
    rb = swap(pb, LAT_B)
    g1, rt, rf = call(middle_rows, (shape(*inner), shape(*flat), shape(*flat)), scratch=planes,
                      specs=[VM] * 8, name="middle_rows", flops=10**9, moved=10**6,
                      )(fk, tv, wet, own, v1, v2, v3, gp)
    e4, fb, dd, rfx, qa, qb = call(
        between,
        (shape(4, 80, 128), shape(64, 128), shape(32, 128), shape(*tall), shape(*tall), shape(96, 128)),
        specs=[VM] * 9, name="between", flops=10**7, moved=10**6,
    )(ra, rb, own, fk, fc, rt, rf, both, mx)
    hb = swap(qb, LON_B)
    ha = swap(qa, LON_A)
    g2 = call(outer_rows, shape(512, 128), scratch=planes, specs=[VM] * 6, name="outer_rows",
              flops=5 * 10**8, moved=10**6)(fk, fb, v1, v2, v3, g1)
    return call(
        closing,
        (shape(*cube), shape(*flat), shape(*flat)),
        scratch=(pltpu.VMEM(cube, F32), pltpu.VMEM((2, 64, 128), F32), pltpu.SemaphoreType.DMA((6,))),
        specs=[VM] * 15, out_specs=(HB, HB, HB), name="closing", flops=10**8, moved=3 * 10**6,
    )(qa, qb, ha, hb, rfx, e4, dd, warm, wet, g1, g2, w1, v2, v3, mx)


def solution(mesh):
    wide, flat = P(None, "lat", "lon"), P("lat", "lon")
    return jax.shard_map(
        on_device,
        mesh=mesh,
        in_specs=(wide, flat, flat, wide, flat, P(), P(), P(), P()),
        out_specs=(wide, flat, flat),
        check_vma=False,
    )
```
